256 devices in a mesh: dp: 32 (over z, x_hi, core), tensor: 8 (over x_lo, y).
Axes of the slice: x: 4 (x_hi: 2, x_lo: 2; x = x_hi * 2 + x_lo), y: 4, z: 8, core: 2. Of those that a mesh axis runs over, the one named last changes fastest.
Arguments:
- picture_skip_entries: bfloat16 [8192, 1536], P('dp', 'tensor'), may hold values from -6 to 6
- picture_activations: bfloat16 [8192, 6144], P('dp', 'tensor'), may hold values from -6 to 6
- picture_contract_weights: bfloat16 [6144, 1536], P('tensor'), may hold values from -1 to 1
- picture_embedding_map: bfloat16 [1536, 1536], P('tensor'), may hold values from -1 to 1
- caption_skip_entries: bfloat16 [8192, 1536], P('dp', 'tensor'), may hold values from -6 to 6
- caption_activations: bfloat16 [8192, 6144], P('dp', 'tensor'), may hold values from -6 to 6
- caption_contract_weights: bfloat16 [6144, 1536], P('tensor'), may hold values from -1 to 1
- caption_embedding_map: bfloat16 [1536, 1536], P('tensor'), may hold values from -1 to 1
- sharpness_coefficient: float32 [1], replicated, may hold values from 5 to 12
- pairwise_score_shift: float32 [1], replicated, may hold values from -4 to -1
Outputs:
- grad_image_proj: float32 [1536, 1536], P('tensor', 'dp')
- grad_text_proj: float32 [1536, 1536], P('tensor', 'dp')
The draws below stay inside these ranges and needn't reach their ends.
All inputs are finite; a program needn't handle non-finite values.
Results may differ from the reference program's by a relative error of at most 0.007.
Values may be sent and summed in bfloat16 or wider, within the bound.
A program may use at most 64 MiB of HBM per device.

```python
import math
import jax
import jax.numpy as jnp
from jax import lax

D = 1536
FF = 6144
E = 1536
B_DEV = 256
BATCH = 8192
N_DP = 32
N_TENSOR = 8


def shared_rows(key, seed_tag, feature_count, cycle_weight):
    shard_count = BATCH // B_DEV
    shard_of_row = (jnp.arange(BATCH, dtype=jnp.int32) // B_DEV).astype(jnp.float32)
    angle = 2.0 * math.pi / shard_count * shard_of_row
    basis = jax.random.normal(jax.random.fold_in(key, seed_tag), (4, feature_count), jnp.float32)
    first_wave = jnp.cos(angle)[:, None] * basis[0][None, :] + jnp.sin(angle)[:, None] * basis[1][None, :]
    second_wave = jnp.cos(2.0 * angle)[:, None] * basis[2][None, :] + jnp.sin(2.0 * angle)[:, None] * basis[3][None, :]
    paired = jax.random.normal(jax.random.fold_in(key, seed_tag + 1), (BATCH, feature_count), jnp.float32)
    return math.sqrt(cycle_weight / 2.0) * (first_wave + second_wave) + math.sqrt(0.9 - cycle_weight) * paired


def shared_matrix(key, seed_tag, row_count, col_count):
    return jax.random.normal(jax.random.fold_in(key, seed_tag), (row_count, col_count), jnp.float32)


def finish_rows(common, private):
    return jnp.clip(common + math.sqrt(0.1) * private, -6.0, 6.0).astype(jnp.bfloat16)


def finish_matrix(common, private, shared_weight, fan_in):
    blended = math.sqrt(shared_weight) * common + math.sqrt(1.0 - shared_weight) * private
    return (jnp.clip(blended, -6.0, 6.0) / math.sqrt(fan_in)).astype(jnp.bfloat16)


def draw_picture_skip_entries(key, part):
    common = shared_rows(key, 200, D, 0.4)
    private = jax.random.normal(jax.random.fold_in(key, 1), (BATCH, D), jnp.float32)
    return finish_rows(common, private)


def draw_picture_activations(key, part):
    common = shared_rows(key, 210, FF, 0.4)
    private = jax.random.normal(jax.random.fold_in(key, 2), (BATCH, FF), jnp.float32)
    return finish_rows(common, private)


def draw_picture_contract_weights(key, part):
    common = shared_matrix(key, 300, FF, D)
    private = jax.random.normal(jax.random.fold_in(key, 3), (FF, D), jnp.float32)
    return finish_matrix(common, private, 0.9, FF)


def draw_picture_embedding_map(key, part):
    common = shared_matrix(key, 310, D, E)
    private = jax.random.normal(jax.random.fold_in(key, 4), (D, E), jnp.float32)
    return finish_matrix(common, private, 0.9, D)


def draw_caption_skip_entries(key, part):
    common = shared_rows(key, 200, D, 0.4)
    private = jax.random.normal(jax.random.fold_in(key, 5), (BATCH, D), jnp.float32)
    return finish_rows(common, private)


def draw_caption_activations(key, part):
    common = shared_rows(key, 210, FF, 0.4)
    private = jax.random.normal(jax.random.fold_in(key, 6), (BATCH, FF), jnp.float32)
    return finish_rows(common, private)


def draw_caption_contract_weights(key, part):
    common = shared_matrix(key, 300, FF, D)
    private = jax.random.normal(jax.random.fold_in(key, 7), (FF, D), jnp.float32)
    return finish_matrix(common, private, 0.9, FF)


def draw_caption_embedding_map(key, part):
    common = shared_matrix(key, 310, D, E)
    private = jax.random.normal(jax.random.fold_in(key, 8), (D, E), jnp.float32)
    return finish_matrix(common, private, 0.9, D)


def setup_inputs(seed: int = 0) -> dict:
    keys = jax.random.split(jax.random.key(seed), 11)
    return {
        "picture_skip_entries": draw_picture_skip_entries(jax.random.fold_in(keys[10], 71), 0),
        "picture_activations": draw_picture_activations(jax.random.fold_in(keys[10], 71), 0),
        "picture_contract_weights": draw_picture_contract_weights(jax.random.fold_in(keys[10], 71), 0),
        "picture_embedding_map": draw_picture_embedding_map(jax.random.fold_in(keys[10], 71), 0),
        "caption_skip_entries": draw_caption_skip_entries(jax.random.fold_in(keys[10], 71), 0),
        "caption_activations": draw_caption_activations(jax.random.fold_in(keys[10], 71), 0),
        "caption_contract_weights": draw_caption_contract_weights(jax.random.fold_in(keys[10], 71), 0),
        "caption_embedding_map": draw_caption_embedding_map(jax.random.fold_in(keys[10], 71), 0),
        "sharpness_coefficient": jnp.clip(jax.random.uniform(keys[8], (1,), jnp.float32, 5.0, 12.0), 5.0, 12.0),
        "pairwise_score_shift": jnp.clip(jax.random.uniform(keys[9], (1,), jnp.float32, -4.0, -1.0), -4.0, -1.0),
    }


def tower(resid, hidden, down_weight, proj_weight):
    ff_part = FF // N_TENSOR
    d_part = D // N_TENSOR
    summed = jnp.zeros((BATCH, D), jnp.float32)
    for shard_index in range(N_TENSOR):
        partial_value = jnp.dot(hidden[:, shard_index * ff_part:(shard_index + 1) * ff_part], down_weight[shard_index * ff_part:(shard_index + 1) * ff_part], preferred_element_type=jnp.float32)
        summed = summed + lax.optimization_barrier(partial_value.astype(jnp.bfloat16)).astype(jnp.float32)
    stream = (resid.astype(jnp.float32) + summed).astype(jnp.bfloat16)
    raw_embed = jnp.zeros((BATCH, E), jnp.float32)
    for shard_index in range(N_TENSOR):
        partial_value = jnp.dot(stream[:, shard_index * d_part:(shard_index + 1) * d_part], proj_weight[shard_index * d_part:(shard_index + 1) * d_part], preferred_element_type=jnp.float32)
        raw_embed = raw_embed + lax.optimization_barrier(partial_value.astype(jnp.bfloat16)).astype(jnp.float32)
    row_norm = jnp.sqrt(lax.optimization_barrier(jnp.sum(raw_embed * raw_embed, axis=1, keepdims=True)) + 1e-06)
    unit_embed = raw_embed / row_norm
    return (stream, unit_embed, row_norm, unit_embed.astype(jnp.bfloat16))

def raw_gradient(grad_embed, unit_embed, row_norm):
    along_unit = lax.optimization_barrier(jnp.sum(unit_embed * grad_embed, axis=1, keepdims=True))
    return ((grad_embed - unit_embed * along_unit) / row_norm).astype(jnp.bfloat16)

def reference(picture_skip_entries, picture_activations, picture_contract_weights, picture_embedding_map, caption_skip_entries, caption_activations, caption_contract_weights, caption_embedding_map, sharpness_coefficient, pairwise_score_shift):
    image_stream, image_unit, image_norm, image_embed = tower(picture_skip_entries, picture_activations, picture_contract_weights, picture_embedding_map)
    text_stream, text_unit, text_norm, text_embed = tower(caption_skip_entries, caption_activations, caption_contract_weights, caption_embedding_map)
    pairwise_score_multiplier = sharpness_coefficient[0]
    logit_shift = pairwise_score_shift[0]
    text_index = jnp.arange(BATCH, dtype=jnp.int32)

    def block_pass(text_grad, block_index):
        first_row = (block_index * B_DEV).astype(jnp.int32)
        picked = lax.dynamic_slice_in_dim(image_embed, first_row, B_DEV, 0)
        logits = pairwise_score_multiplier * jnp.dot(picked, text_embed.T, preferred_element_type=jnp.float32) + logit_shift
        image_index = first_row + jnp.arange(B_DEV, dtype=jnp.int32)
        positive = image_index[:, None] == text_index[None, :]
        pair_coef = (pairwise_score_multiplier * (jax.nn.sigmoid(logits) - positive.astype(jnp.float32))).astype(jnp.bfloat16)
        image_block = jnp.dot(pair_coef, text_embed, preferred_element_type=jnp.float32)
        text_grad = text_grad + jnp.dot(pair_coef.T, picked, preferred_element_type=jnp.float32)
        return (text_grad, image_block)
    text_grad, image_blocks = lax.scan(block_pass, jnp.zeros((BATCH, E), jnp.float32), jnp.arange(N_DP, dtype=jnp.int32))
    image_grad = image_blocks.reshape(BATCH, E)
    image_raw = raw_gradient(image_grad, image_unit, image_norm)
    text_raw = raw_gradient(text_grad, text_unit, text_norm)
    grad_image_proj = jnp.dot(image_stream.T, image_raw, preferred_element_type=jnp.float32)
    grad_text_proj = jnp.dot(text_stream.T, text_raw, preferred_element_type=jnp.float32)
    return (grad_image_proj, grad_text_proj)
```

```python
from types import SimpleNamespace

import jax
import jax.numpy as jnp
from jax import lax
from jax.experimental import pallas as pl
from jax.experimental.pallas import tpu as pltpu
from jax.sharding import PartitionSpec as P

MESH = pl.DeviceIdType.MESH
BF16, F32 = jnp.bfloat16, jnp.float32
VMEM_LIMIT = 60 * 1024 * 1024


def device(z, x, y, c):
    return (z * 4 + x // 2 * 2 + c, x % 2 * 4 + y)


def push(src, dst, send, recv, peer):
    copy = pltpu.make_async_remote_copy(
        src_ref=src, dst_ref=dst, send_sem=send, recv_sem=recv, device_id=peer, device_id_type=MESH
    )
    copy.start()
    return copy


def raw_gradient(grad, unit, norm):
    along = jnp.sum(unit * grad, axis=1, keepdims=True)
    return ((grad - unit * along) / norm).astype(BF16)


def scatter_scratch(one, other):
    return dict(
        one=pltpu.VMEM((2, 8, *one), BF16),
        other=pltpu.VMEM((2, 8, *other), BF16),
        cross_in=pltpu.VMEM((2, 4, *one), BF16),
        half_out=pltpu.VMEM((2, 4, *one), BF16),
        half_in=pltpu.VMEM((2, 4, *one), BF16),
        round_out=pltpu.VMEM((2, 2, *other), BF16),
        round_in=pltpu.VMEM((2, 6, *other), BF16),
        wide_out=pltpu.VMEM((2, 2, *other), BF16),
        wide_in=pltpu.VMEM((2, *other), BF16),
        sem=pltpu.SemaphoreType.DMA((2, 2, 12)),
    )


DOWN = scatter_scratch((80, 256), (112, 256))
EMB = scatter_scratch((32, 640), (32, 896))
SCRATCH = dict(
    act=pltpu.VMEM((2, 256, 768), BF16),
    w=pltpu.VMEM((2, 768, 1536), BF16),
    m=pltpu.VMEM((2, 192, 1536), BF16),
    skip=pltpu.VMEM((2, 192, 256), BF16),
    stream=pltpu.VMEM((8, 2, 192, 256), BF16),
    unit=pltpu.VMEM((2, 32, 1536), F32),
    norm=pltpu.VMEM((2, 32, 128), F32),
    img=pltpu.VMEM((2, 4, 4, 16, 1536), BF16),
    txt=pltpu.VMEM((2, 8, 32, 1536), BF16),
    coef=pltpu.VMEM((2, 256, 512), BF16),
    coef_t=pltpu.VMEM((2, 256, 512), BF16),
    gt_own=pltpu.VMEM((8, 32, 1536), F32),
    gt_out=pltpu.VMEM((8, 32, 1536), BF16),
    gt_in=pltpu.VMEM((8, 32, 1536), BF16),
    gz_out=pltpu.VMEM((8, 32, 1536), BF16),
    gz_in=pltpu.VMEM((8, 32, 1536), BF16),
    gi_out=pltpu.VMEM((2, 4, 4, 16, 1536), BF16),
    gi_in=pltpu.VMEM((2, 4, 4, 16, 1536), BF16),
    gh_out=pltpu.VMEM((2, 4, 16, 1536), BF16),
    gh_in=pltpu.VMEM((2, 4, 16, 1536), BF16),
    pack=pltpu.VMEM((2, 8, 16, 384), BF16),
    graw=pltpu.VMEM((2, 8, 8, 16, 384), BF16),
    part=pltpu.VMEM((2, 2, 48, 384), F32),
    part_in=pltpu.VMEM((2, 48, 384), F32),
    last_out=pltpu.VMEM((48, 384), F32),
    last_in=pltpu.VMEM((48, 384), F32),
    load_sem=pltpu.SemaphoreType.DMA((2, 7)),
    stream_sem=pltpu.SemaphoreType.DMA((2, 9)),
    img_sem=pltpu.SemaphoreType.DMA((2, 3, 2, 4)),
    txt_sem=pltpu.SemaphoreType.DMA((2, 8, 2)),
    pair_sem=pltpu.SemaphoreType.DMA((2, 8)),
    gt_sem=pltpu.SemaphoreType.DMA((2,)),
    gz_sem=pltpu.SemaphoreType.DMA((2, 8, 2)),
    gi_sem=pltpu.SemaphoreType.DMA((2, 3, 2, 4)),
    turn_sem=pltpu.SemaphoreType.DMA((2, 2, 8)),
    spread_sem=pltpu.SemaphoreType.DMA((2, 2, 3, 8)),
    part_sem=pltpu.SemaphoreType.DMA((2, 2)),
)


def window_kernel(*refs):
    inputs, (scale_ref, shift_ref), output = refs[:8], refs[8:10], refs[10]
    count = len(SCRATCH)
    v = SimpleNamespace(**dict(zip(SCRATCH, refs[11:])))
    v.down = SimpleNamespace(**dict(zip(DOWN, refs[11 + count :])))
    v.emb = SimpleNamespace(**dict(zip(EMB, refs[11 + count + len(DOWN) :])))
    for s in (v.down, v.emb):
        s.relay, s.cross, s.near, s.last, s.along, s.wide = ({} for _ in range(6))
    d, t = lax.axis_index("dp"), lax.axis_index("tensor")
    z, x, y, c = d // 4, d // 2 % 2 * 2 + t // 4, t % 4, d % 2
    sends = []

    def send(*args):
        copy = push(*args)
        sends.append(copy)
        return copy

    def to_x(k):
        return device(z, (x + k) % 4, y, c)

    def to_y(k):
        return (d, t // 4 * 4 + (y + k) % 4)

    def to_z(k):
        return ((z + k) % 8 * 4 + d % 4, t)

    sibling = (d // 2 * 2 + 1 - c, t)

    loads = {}
    for tower in (1, 0):
        act, w, m, skip = inputs[tower * 4 : tower * 4 + 4]
        pairs = [(act, v.act.at[tower])]
        for f in range(4):
            cols = pl.ds(f * 384, 384)
            pairs.append((w.at[:, cols], v.w.at[tower, :, cols]))
        pairs += [(m, v.m.at[tower]), (skip, v.skip.at[tower])]
        row = []
        for j, (source, target) in enumerate(pairs):
            load = pltpu.make_async_copy(source, target, v.load_sem.at[tower, j])
            load.start()
            row.append(load)
        loads[tower] = row

    peers = [(d, (t + k) % 8) for k in range(1, 8)]
    peers += [to_z(k) for k in range(1, 8)]
    peers += [device(z, (x + 2) % 4, y, c), device(z, (x // 2 * 2 + 2) % 4 + 1 - x % 2, y, c)]
    peers += [sibling]
    barrier = pltpu.get_barrier_semaphore()
    for peer in peers:
        pl.semaphore_signal(barrier, inc=1, device_id=peer, device_id_type=MESH)

    low = t // 4
    partner = (d, (t + 4) % 8)

    def scatter_start(s, tower):
        def hop(j, k, wide, way):
            return send(
                s.other.at[tower, wide * 4 + (y + k) % 4],
                s.round_in.at[tower, j],
                s.sem.at[0, tower, j],
                s.sem.at[1, tower, j],
                to_y(way),
            )

        s.relay[tower] = [hop(0, 2, 0, 1), hop(1, 2, 1, -1)]
        s.cross[tower] = send(
            s.one.at[tower, pl.ds((1 - low) * 4, 4)],
            s.cross_in.at[tower],
            s.sem.at[0, tower, 6],
            s.sem.at[1, tower, 6],
            partner,
        )
        s.near[tower] = [hop(2, 1, 1, 1), hop(3, 3, 0, -1)]

    def half_sum(s, tower, k):
        place = (y + k) % 4
        return s.one[tower, low * 4 + place].astype(F32) + s.cross_in[tower, place].astype(F32)

    def scatter_relay(s, tower):
        s.last[tower] = []
        for j, way in ((0, 1), (1, -1)):
            s.relay[tower][j].wait_recv()
            total = s.other[tower, j * 4 + (y + way) % 4].astype(F32)
            total += s.round_in[tower, j].astype(F32)
            s.round_out[tower, j] = total.astype(BF16)
            s.last[tower].append(
                send(
                    s.round_out.at[tower, j],
                    s.round_in.at[tower, 4 + j],
                    s.sem.at[0, tower, 4 + j],
                    s.sem.at[1, tower, 4 + j],
                    to_y(way),
                )
            )

    def scatter_along(s, tower):
        s.cross[tower].wait_recv()
        s.along[tower] = []
        for k in (2, 1, 3):
            s.half_out[tower, k] = half_sum(s, tower, k).astype(BF16)
            s.along[tower].append(
                send(
                    s.half_out.at[tower, k],
                    s.half_in.at[tower, k],
                    s.sem.at[0, tower, 7 + k],
                    s.sem.at[1, tower, 7 + k],
                    to_y(k),
                )
            )

    def scatter_wide(s, tower):
        for j in range(2):
            s.near[tower][1 - j].wait_recv()
            s.last[tower][j].wait_recv()
            total = s.other[tower, j * 4 + y].astype(F32)
            total += s.round_in[tower, 3 - j].astype(F32)
            total += s.round_in[tower, 4 + j].astype(F32)
            s.wide_out[tower, j] = total.astype(BF16)
        s.wide[tower] = send(
            s.wide_out.at[tower, 1 - low],
            s.wide_in.at[tower],
            s.sem.at[0, tower, 11],
            s.sem.at[1, tower, 11],
            partner,
        )

    def scatter_end(s, tower, axis):
        first = half_sum(s, tower, 0)
        for k in (1, 3, 2):
            s.along[tower][(2, 1, 3).index(k)].wait_recv()
            first += s.half_in[tower, k].astype(F32)
        s.wide[tower].wait_recv()
        second = s.wide_out[tower, low].astype(F32) + s.wide_in[tower].astype(F32)
        return jnp.concatenate([first, second], axis=axis)

    def down_projection(tower):
        loads[tower][0].wait()
        for f in range(4):
            loads[tower][1 + f].wait()
            product = jnp.dot(
                v.act[tower], v.w[tower, :, f * 384 : f * 384 + 384], preferred_element_type=F32
            )
            product = product.T.reshape(2, 192, 256).astype(BF16)
            v.down.one[tower, 2 * f : 2 * f + 2] = product[:, :80]
            v.down.other[tower, 2 * f : 2 * f + 2] = product[:, 80:]

        if tower == 1:
            pl.semaphore_wait(barrier, len(peers))
        scatter_start(v.down, tower)

    source = lax.broadcasted_iota(jnp.int32, (256, 256), 0)
    target = lax.broadcasted_iota(jnp.int32, (256, 256), 1)
    wanted = (target & 112) * 2 + (target & 15) + lax.shift_right_logical(target & 128, 3)
    reorder = (source == wanted).astype(F32).astype(BF16)

    def embedding_projection(tower):
        loads[tower][5].wait()
        loads[tower][6].wait()
        total = v.skip[tower].astype(F32) + scatter_end(v.down, tower, 0)
        columns = total.astype(BF16)
        rows = columns.T

        for f in range(6):
            product = jnp.dot(
                rows, v.m[tower, :, f * 256 : f * 256 + 256], preferred_element_type=F32
            )
            product = product.reshape(8, 32, 256).astype(BF16)
            cut = min(max(640 - f * 256, 0), 256)
            if cut > 0:
                v.emb.one[tower, :, :, f * 256 : f * 256 + cut] = product[:, :, :cut]
            if cut < 256:
                start = f * 256 + cut - 640
                v.emb.other[tower, :, :, start : start + 256 - cut] = product[:, :, cut:]

        scatter_start(v.emb, tower)
        v.stream[0, tower] = jnp.dot(columns, reorder, preferred_element_type=F32).astype(BF16)

    def await_all(copies):
        for copy in copies:
            copy.wait_recv()

    def stream_step(step):
        if step < 4:
            ways = ((1, (step - 1,), (step,), step), (-1, ((9 - step) % 8,), (8 - step,), 8 - step))
        else:
            ways = ((1, (3, 0), (4, 0), 4), (-1, (5, 1), (4, 1), 8))
        return [
            send(
                v.stream.at[at], v.stream.at[to], v.stream_sem.at[0, j], v.stream_sem.at[1, j], to_z(way)
            )
            for way, at, to, j in ways
        ]

    first, second = 1, 0
    down_projection(first)
    down_projection(second)
    scatter_relay(v.down, first)
    scatter_along(v.down, first)
    scatter_relay(v.down, second)
    scatter_wide(v.down, first)
    scatter_along(v.down, second)
    scatter_wide(v.down, second)
    embedding_projection(first)
    embedding_projection(second)
    stream_ring = stream_step(1)
    scatter_relay(v.emb, first)
    scatter_along(v.emb, first)
    scatter_relay(v.emb, second)
    scatter_wide(v.emb, first)
    scatter_along(v.emb, second)
    scatter_wide(v.emb, second)
    await_all(stream_ring)
    stream_ring = stream_step(2)

    def embed(tower):
        raw = scatter_end(v.emb, tower, 1)
        norm = jnp.sqrt(jnp.sum(raw * raw, axis=1, keepdims=True) + 1e-06)
        unit = raw / norm
        v.unit[tower] = unit
        v.norm[tower] = jnp.broadcast_to(norm, (32, 128))
        return unit.astype(BF16)

    v.txt[0, 0] = embed(1)
    pair_copies = []
    txt_copies = {}

    def share(slot):
        pair_copies.append(
            send(v.txt.at[0, slot], v.txt.at[1, slot], v.pair_sem.at[0, slot], v.pair_sem.at[1, slot], sibling)
        )

    def txt_step(step):
        up, down = (step - 1, step, 1), ((9 - step) % 8, 8 - step, -1)
        for (at, to, way), half in ((up, 0), (down, 1), (up, 1), (down, 0)):
            if at != 0:
                txt_copies[at, half].wait_recv()
            if to != 4 or half == (way < 0):
                rows = pl.ds(half * 16, 16)
                txt_copies[to, half] = send(
                    v.txt.at[0, at, rows],
                    v.txt.at[0, to, rows],
                    v.txt_sem.at[0, to, half],
                    v.txt_sem.at[1, to, half],
                    to_z(way),
                )
        for at in {up[0], down[0]}:
            share(at)

    txt_step(1)

    unit = embed(0)
    v.img[0, 0, 0] = unit[:16]
    v.img[1, 0, 0] = unit[16:]
    ways = (to_x, to_y)

    def image_push(at, to, phase, half, k, way):
        sem = v.img_sem
        return send(
            v.img.at[at], v.img.at[to], sem.at[0, phase, half, k], sem.at[1, phase, half, k], way(k)
        )

    img_first = ([], [])
    img_copies = []
    for k in (2, 1, 3):
        for half in range(2):
            img_first[half].append(image_push((half, 0, 0), (half, 0, k), 0, half, k, ways[half]))
    for k in (2, 1, 3):
        for half in range(2):
            img_copies.append(image_push((half, 0, 0), (half, k, 0), 1, half, k, ways[1 - half]))

    txt_step(2)
    txt_step(3)
    turned = pl.ds(1, 3)
    for half in range(2):
        await_all(img_first[half])
        for k in (2, 1, 3):
            img_copies.append(
                image_push((half, 0, turned), (half, k, turned), 2, half, k, ways[1 - half])
            )
    txt_step(4)
    await_all(txt_copies[4, half] for half in range(2))
    share(4)
    await_all(stream_ring)
    stream_ring = stream_step(3)
    await_all(img_copies)

    scale, shift = scale_ref[0], shift_ref[0]
    row_id = lax.broadcasted_iota(jnp.int32, (256, 256), 0)
    col_id = lax.broadcasted_iota(jnp.int32, (256, 256), 1)

    def pair_coefficients(core):
        @pl.loop(0, 2, unroll=True)
        def _(half):
            inner = lax.dot_general(
                v.img[half].reshape(256, 1536),
                v.txt[core].reshape(256, 1536),
                (((1,), (1,)), ((), ())),
                preferred_element_type=F32,
            )
            value = jax.nn.sigmoid(scale * inner + shift)
            if core == 0:
                positive = (row_id < 16) & (row_id + half * 16 == col_id)
                value = value - positive.astype(F32)
            value = scale * value
            v.coef[half, :, core * 256 : core * 256 + 256] = value.astype(BF16)
            v.coef_t[core, :, pl.ds(pl.multiple_of(half * 256, 256), 256)] = value.T.astype(BF16)

    pair_coefficients(0)
    await_all(pair_copies)
    pair_coefficients(1)

    def text_partials(core):
        @pl.loop(0, 6, unroll=True)
        def _(f):
            cols = pl.ds(pl.multiple_of(f * 256, 256), 256)
            product = jnp.dot(
                v.coef_t[core], v.img[:, :, :, :, cols].reshape(512, 256), preferred_element_type=F32
            ).reshape(8, 32, 256)
            if core == 0:
                v.gt_own[:, :, cols] = product
            else:
                v.gt_out[:, :, cols] = product.astype(BF16)

    def image_partials(half):
        @pl.loop(0, 6, unroll=True)
        def _(f):
            cols = pl.ds(pl.multiple_of(f * 256, 256), 256)
            product = jnp.dot(
                v.coef[half], v.txt[:, :, :, cols].reshape(512, 256), preferred_element_type=F32
            )
            v.gi_out[half, :, :, :, cols] = product.reshape(4, 4, 16, 256).astype(BF16)

    gi_first, gi_copies = ([], []), ([], [])

    def image_start(half):
        image_partials(half)
        for phase, blocks, copies in ((0, turned, gi_first), (2, pl.ds(0, 1), gi_copies)):
            for k in (2, 1, 3):
                copies[half].append(
                    send(
                        v.gi_out.at[half, k, blocks],
                        v.gi_in.at[half, k, blocks],
                        v.gi_sem.at[0, phase, half, k],
                        v.gi_sem.at[1, phase, half, k],
                        ways[1 - half](-k),
                    )
                )

    gh_copies = ([], [])

    def image_own(half, k):
        total = v.gi_out[half, 0, k].astype(F32)
        for j in range(1, 4):
            total += v.gi_in[half, j, k].astype(F32)
        return total

    def image_middle(half):
        await_all(gi_first[half])
        for k in (2, 1, 3):
            v.gh_out[half, k] = image_own(half, k).astype(BF16)
            gh_copies[half].append(
                send(
                    v.gh_out.at[half, k],
                    v.gh_in.at[half, k],
                    v.gi_sem.at[0, 1, half, k],
                    v.gi_sem.at[1, 1, half, k],
                    ways[half](-k),
                )
            )

    def image_end(half):
        await_all(gi_copies[half])
        total = image_own(half, 0)
        await_all(gh_copies[half])
        for k in range(1, 4):
            total += v.gh_in[half, k].astype(F32)
        return total

    gz_copies = {}

    def text_own(r, half):
        rows = slice(half * 16, half * 16 + 16)
        return v.gt_own[r, rows] + v.gt_in[r, rows].astype(F32)

    def text_step(step):
        moves = [(5 - step, 0, -1), (3 + step, 1, 1)]
        if step < 4:
            moves += [(4 - step, 1, -1), (4 + step, 0, 1)]
        for r, half, way in moves:
            rows = slice(half * 16, half * 16 + 16)
            total = text_own(r, half)
            before = r - way
            if (before, half) in gz_copies and (before != 4 or half == (way > 0)):
                gz_copies[before, half].wait_recv()
                total += v.gz_in[before, rows].astype(F32)
            v.gz_out[r, rows] = total.astype(BF16)
            gz_copies[r, half] = send(
                v.gz_out.at[r, pl.ds(half * 16, 16)],
                v.gz_in.at[r, pl.ds(half * 16, 16)],
                v.gz_sem.at[0, r, half],
                v.gz_sem.at[1, r, half],
                to_z(way),
            )

    def text_end(half):
        rows = slice(half * 16, half * 16 + 16)
        total = text_own(0, half)
        for r in (1, 7):
            gz_copies[r, half].wait_recv()
            total += v.gz_in[r, rows].astype(F32)
        return total

    text_partials(1)
    gt_copy = send(v.gt_out, v.gt_in, v.gt_sem.at[0], v.gt_sem.at[1], sibling)
    image_start(0)
    image_start(1)
    text_partials(0)
    gt_copy.wait_recv()
    text_step(1)
    text_step(2)
    text_step(3)
    image_middle(0)
    image_middle(1)
    text_step(4)

    turn_copies = ([], [])

    def turn(tower, grad):
        raw = raw_gradient(grad, v.unit[tower], v.norm[tower][:, :1])
        for k in range(8):
            cols = slice(k * 192, k * 192 + 192)
            v.pack[tower, k] = jnp.concatenate([raw[:16, cols], raw[16:, cols]], axis=1)
        v.graw[tower, t, 0] = v.pack[tower, z]
        for k in range(1, 8):
            turn_copies[tower].append(
                send(
                    v.pack.at[tower, (z + k) % 8],
                    v.graw.at[tower, t, k],
                    v.turn_sem.at[0, tower, k],
                    v.turn_sem.at[1, tower, k],
                    to_z(k),
                )
            )

    turn(1, jnp.concatenate([text_end(half) for half in range(2)], axis=0))
    turn(0, jnp.concatenate([image_end(half) for half in range(2)], axis=0))

    spread_copies, low_copies, high_copies = ([], []), {}, {}

    low_slots, high_slots = pl.ds(0, 3), pl.ds(3, 5)

    def spread(tower, owner, slots, phase, j, peer):
        block = v.graw.at[tower, owner, slots]
        sem = v.spread_sem
        return send(block, block, sem.at[0, tower, phase, j], sem.at[1, tower, phase, j], peer)

    def spread_start(tower):
        await_all(turn_copies[tower][:2])
        low_copies[tower] = spread(tower, t, low_slots, 0, 0, partner)
        await_all(turn_copies[tower][2:])
        high_copies[tower] = [spread(tower, t, high_slots, 0, k, to_y(k)) for k in range(1, 4)]
        spread_copies[tower].append(spread(tower, t, high_slots, 1, 0, partner))
        spread_copies[tower].extend(
            spread(tower, t, low_slots, 1, k, to_y(k)) for k in range(1, 4)
        )

    def spread_end(tower):
        low_copies[tower].wait_recv()
        for k in range(1, 4):
            spread_copies[tower].append(
                spread(tower, (t + 4) % 8, low_slots, 2, k, to_y(k))
            )
        for k in (1, 3, 2):
            high_copies[tower][k - 1].wait_recv()
            owner = low * 4 + (y - k) % 4
            spread_copies[tower].append(spread(tower, owner, high_slots, 2, k + 4, partner))

    def contract(tower):
        await_all(spread_copies[tower])
        totals = [jnp.zeros((192, 256), F32)] * 2
        for r in range(0, 8, 2):
            rows = jnp.concatenate([v.graw[tower, :, r + i].reshape(128, 384) for i in range(2)], axis=0)
            for half in range(2):
                lanes = slice(half * 128, half * 128 + 128)
                columns = jnp.concatenate([v.stream[r + i, tower, :, lanes] for i in range(2)], axis=1)
                totals[half] += jnp.dot(
                    columns, rows[:, half * 128 : half * 128 + 256], preferred_element_type=F32
                )
        return (totals[0][:, :192] + totals[1][:, 64:]).T

    await_all(stream_ring)
    stream_ring = stream_step(4)
    spread_start(first)
    spread_start(second)
    spread_end(first)
    spread_end(second)
    await_all(stream_ring)
    text_sum = contract(1)
    sums = jnp.concatenate([contract(0), text_sum], axis=1)
    for q in range(4):
        v.part[q % 2, q // 2] = sums[q * 48 : q * 48 + 48]

    core_copy = send(v.part.at[1 - c], v.part_in, v.part_sem.at[0, 0], v.part_sem.at[1, 0], sibling)
    high = x // 2
    core_copy.wait_recv()
    v.last_out[...] = v.part[c, 1 - high] + v.part_in[1 - high]
    last_copy = send(
        v.last_out, v.last_in, v.part_sem.at[0, 1], v.part_sem.at[1, 1], device(z, (x + 2) % 4, y, c)
    )
    total = v.part[c, high] + v.part_in[high]
    last_copy.wait_recv()
    output[...] = total + v.last_in[...]
    for copy in sends:
        copy.wait_send()


def on_device(
    picture_skip_entries,
    picture_activations,
    picture_contract_weights,
    picture_embedding_map,
    caption_skip_entries,
    caption_activations,
    caption_contract_weights,
    caption_embedding_map,
    sharpness_coefficient,
    pairwise_score_shift,
):
    both = pl.pallas_call(
        window_kernel,
        out_shape=jax.ShapeDtypeStruct((48, 384), F32),
        in_specs=[pl.BlockSpec(memory_space=pl.ANY)] * 8
        + [pl.BlockSpec(memory_space=pltpu.SMEM)] * 2,
        out_specs=pl.BlockSpec(memory_space=pltpu.VMEM),
        scratch_shapes=[*SCRATCH.values(), *DOWN.values(), *EMB.values()],
        compiler_params=pltpu.CompilerParams(
            collective_id=0, has_side_effects=True, vmem_limit_bytes=VMEM_LIMIT
        ),
    )(
        picture_activations,
        picture_contract_weights,
        picture_embedding_map,
        picture_skip_entries.T,
        caption_activations,
        caption_contract_weights,
        caption_embedding_map,
        caption_skip_entries.T,
        sharpness_coefficient,
        pairwise_score_shift,
    )
    return both[:, :192].T, both[:, 192:].T


def solution(mesh):
    placed = (
        P("dp", "tensor"),
        P("dp", "tensor"),
        P("tensor", None),
        P("tensor", None),
        P("dp", "tensor"),
        P("dp", "tensor"),
        P("tensor", None),
        P("tensor", None),
        P(),
        P(),
    )
    return jax.shard_map(
        on_device,
        mesh=mesh,
        in_specs=placed,
        out_specs=(P("tensor", "dp"), P("tensor", "dp")),
        check_vma=False,
    )
```

```python
from types import SimpleNamespace

import jax
import jax.numpy as jnp
from jax import lax
from jax.experimental import pallas as pl
from jax.experimental.pallas import tpu as pltpu
from jax.sharding import PartitionSpec as P

MESH = pl.DeviceIdType.MESH
BF16, F32 = jnp.bfloat16, jnp.float32
VMEM_LIMIT = 60 * 1024 * 1024


def device(z, x, y, c):
    return (z * 4 + x // 2 * 2 + c, x % 2 * 4 + y)


def push(src, dst, send, recv, peer):
    copy = pltpu.make_async_remote_copy(
        src_ref=src, dst_ref=dst, send_sem=send, recv_sem=recv, device_id=peer, device_id_type=MESH
    )
    copy.start()
    return copy


def raw_gradient(grad, unit, norm):
    along = jnp.sum(unit * grad, axis=1, keepdims=True)
    return ((grad - unit * along) / norm).astype(BF16)


def scatter_scratch(one, other):
    return dict(
        one=pltpu.VMEM((2, 8, *one), BF16),
        other=pltpu.VMEM((2, 8, *other), BF16),
        cross_in=pltpu.VMEM((2, 4, *one), BF16),
        half_out=pltpu.VMEM((2, 4, *one), BF16),
        half_in=pltpu.VMEM((2, 4, *one), BF16),
        round_out=pltpu.VMEM((2, 2, *other), BF16),
        round_in=pltpu.VMEM((2, 6, *other), BF16),
        wide_out=pltpu.VMEM((2, 2, *other), BF16),
        wide_in=pltpu.VMEM((2, *other), BF16),
        sem=pltpu.SemaphoreType.DMA((2, 2, 12)),
    )


DOWN = scatter_scratch((80, 256), (112, 256))
EMB = scatter_scratch((32, 640), (32, 896))
SCRATCH = dict(
    act=pltpu.VMEM((2, 256, 768), BF16),
    w=pltpu.VMEM((2, 768, 1536), BF16),
    m=pltpu.VMEM((2, 192, 1536), BF16),
    skip=pltpu.VMEM((2, 192, 256), BF16),
    stream=pltpu.VMEM((8, 2, 192, 256), BF16),
    unit=pltpu.VMEM((2, 32, 1536), F32),
    norm=pltpu.VMEM((2, 32, 128), F32),
    img=pltpu.VMEM((2, 4, 4, 16, 1536), BF16),
    txt=pltpu.VMEM((2, 8, 32, 1536), BF16),
    coef=pltpu.VMEM((2, 256, 512), BF16),
    coef_t=pltpu.VMEM((2, 256, 512), BF16),
    gt_own=pltpu.VMEM((8, 32, 1536), F32),
    gt_out=pltpu.VMEM((8, 32, 1536), BF16),
    gt_in=pltpu.VMEM((8, 32, 1536), BF16),
    gz_out=pltpu.VMEM((8, 32, 1536), BF16),
    gz_in=pltpu.VMEM((8, 32, 1536), BF16),
    gi_out=pltpu.VMEM((2, 4, 4, 16, 1536), BF16),
    gi_in=pltpu.VMEM((2, 4, 4, 16, 1536), BF16),
    gh_out=pltpu.VMEM((2, 4, 16, 1536), BF16),
    gh_in=pltpu.VMEM((2, 4, 16, 1536), BF16),
    pack=pltpu.VMEM((2, 8, 16, 384), BF16),
    graw=pltpu.VMEM((2, 8, 8, 16, 384), BF16),
    part=pltpu.VMEM((2, 4, 48, 256), F32),
    part_in=pltpu.VMEM((2, 4, 48, 256), F32),
    load_sem=pltpu.SemaphoreType.DMA((2, 7)),
    stream_sem=pltpu.SemaphoreType.DMA((2, 9)),
    img_sem=pltpu.SemaphoreType.DMA((2, 3, 2, 4)),
    txt_sem=pltpu.SemaphoreType.DMA((2, 8, 2)),
    pair_sem=pltpu.SemaphoreType.DMA((2, 8)),
    gt_sem=pltpu.SemaphoreType.DMA((2, 3)),
    gz_sem=pltpu.SemaphoreType.DMA((2, 8, 2)),
    gi_sem=pltpu.SemaphoreType.DMA((2, 3, 2, 4)),
    turn_sem=pltpu.SemaphoreType.DMA((2, 2, 8)),
    spread_sem=pltpu.SemaphoreType.DMA((2, 2, 3, 8)),
    part_sem=pltpu.SemaphoreType.DMA((2, 2, 4)),
)


def window_kernel(*refs):
    inputs, (scale_ref, shift_ref), output = refs[:8], refs[8:10], refs[10]
    count = len(SCRATCH)
    v = SimpleNamespace(**dict(zip(SCRATCH, refs[11:])))
    v.down = SimpleNamespace(**dict(zip(DOWN, refs[11 + count :])))
    v.emb = SimpleNamespace(**dict(zip(EMB, refs[11 + count + len(DOWN) :])))
    for s in (v.down, v.emb):
        s.relay, s.cross, s.near, s.last, s.along, s.wide = ({} for _ in range(6))
    d, t = lax.axis_index("dp"), lax.axis_index("tensor")
    z, x, y, c = d // 4, d // 2 % 2 * 2 + t // 4, t % 4, d % 2
    sends, settled = [], [0]

    def send(*args):
        copy = push(*args)
        sends.append(copy)
        return copy

    def settle(mark):
        for copy in sends[settled[0] : mark]:
            copy.wait_send()
        settled[0] = max(settled[0], mark)

    def to_x(k):
        return device(z, (x + k) % 4, y, c)

    def to_y(k):
        return (d, t // 4 * 4 + (y + k) % 4)

    def to_z(k):
        return ((z + k) % 8 * 4 + d % 4, t)

    sibling = (d // 2 * 2 + 1 - c, t)

    loads = {}
    for tower in (1, 0):
        act, w, m, skip = inputs[tower * 4 : tower * 4 + 4]
        pairs = [(act, v.act.at[tower])]
        for f in range(4):
            cols = pl.ds(f * 384, 384)
            pairs.append((w.at[:, cols], v.w.at[tower, :, cols]))
        pairs += [(m, v.m.at[tower]), (skip, v.skip.at[tower])]
        row = []
        for j, (source, target) in enumerate(pairs):
            load = pltpu.make_async_copy(source, target, v.load_sem.at[tower, j])
            load.start()
            row.append(load)
        loads[tower] = row

    peers = [(d, (t + k) % 8) for k in range(1, 8)]
    peers += [to_z(k) for k in range(1, 8)]
    peers += [device(z, (x + 2) % 4, y, c), device(z, (x // 2 * 2 + 2) % 4 + 1 - x % 2, y, c)]
    peers += [sibling, device(z, (x + 2) % 4, y, 1 - c)]
    barrier = pltpu.get_barrier_semaphore()
    for peer in peers:
        pl.semaphore_signal(barrier, inc=1, device_id=peer, device_id_type=MESH)

    low = t // 4
    partner = (d, (t + 4) % 8)

    def scatter_start(s, tower):
        def hop(j, k, wide, way):
            return send(
                s.other.at[tower, wide * 4 + (y + k) % 4],
                s.round_in.at[tower, j],
                s.sem.at[0, tower, j],
                s.sem.at[1, tower, j],
                to_y(way),
            )

        s.relay[tower] = [hop(0, 2, 0, 1), hop(1, 2, 1, -1)]
        s.cross[tower] = send(
            s.one.at[tower, pl.ds((1 - low) * 4, 4)],
            s.cross_in.at[tower],
            s.sem.at[0, tower, 6],
            s.sem.at[1, tower, 6],
            partner,
        )
        s.near[tower] = [hop(2, 1, 1, 1), hop(3, 3, 0, -1)]

    def half_sum(s, tower, k):
        place = (y + k) % 4
        return s.one[tower, low * 4 + place].astype(F32) + s.cross_in[tower, place].astype(F32)

    def scatter_relay(s, tower):
        s.last[tower] = []
        for j, way in ((0, 1), (1, -1)):
            s.relay[tower][j].wait_recv()
            total = s.other[tower, j * 4 + (y + way) % 4].astype(F32)
            total += s.round_in[tower, j].astype(F32)
            s.round_out[tower, j] = total.astype(BF16)
            s.last[tower].append(
                send(
                    s.round_out.at[tower, j],
                    s.round_in.at[tower, 4 + j],
                    s.sem.at[0, tower, 4 + j],
                    s.sem.at[1, tower, 4 + j],
                    to_y(way),
                )
            )

    def scatter_along(s, tower):
        s.cross[tower].wait_recv()
        s.along[tower] = []
        for k in (2, 1, 3):
            s.half_out[tower, k] = half_sum(s, tower, k).astype(BF16)
            s.along[tower].append(
                send(
                    s.half_out.at[tower, k],
                    s.half_in.at[tower, k],
                    s.sem.at[0, tower, 7 + k],
                    s.sem.at[1, tower, 7 + k],
                    to_y(k),
                )
            )

    def scatter_wide(s, tower):
        for j in range(2):
            s.near[tower][1 - j].wait_recv()
            s.last[tower][j].wait_recv()
            total = s.other[tower, j * 4 + y].astype(F32)
            total += s.round_in[tower, 3 - j].astype(F32)
            total += s.round_in[tower, 4 + j].astype(F32)
            s.wide_out[tower, j] = total.astype(BF16)
        s.wide[tower] = send(
            s.wide_out.at[tower, 1 - low],
            s.wide_in.at[tower],
            s.sem.at[0, tower, 11],
            s.sem.at[1, tower, 11],
            partner,
        )

    def scatter_end(s, tower, axis):
        first = half_sum(s, tower, 0)
        for k in (1, 3, 2):
            s.along[tower][(2, 1, 3).index(k)].wait_recv()
            first += s.half_in[tower, k].astype(F32)
        s.wide[tower].wait_recv()
        second = s.wide_out[tower, low].astype(F32) + s.wide_in[tower].astype(F32)
        return jnp.concatenate([first, second], axis=axis)

    def down_projection(tower):
        loads[tower][0].wait()
        for f in range(4):
            loads[tower][1 + f].wait()
            product = jnp.dot(
                v.act[tower], v.w[tower, :, f * 384 : f * 384 + 384], preferred_element_type=F32
            )
            product = product.T.reshape(2, 192, 256).astype(BF16)
            v.down.one[tower, 2 * f : 2 * f + 2] = product[:, :80]
            v.down.other[tower, 2 * f : 2 * f + 2] = product[:, 80:]

        if tower == 1:
            pl.semaphore_wait(barrier, len(peers))
        scatter_start(v.down, tower)

    source = lax.broadcasted_iota(jnp.int32, (256, 256), 0)
    target = lax.broadcasted_iota(jnp.int32, (256, 256), 1)
    wanted = (target & 112) * 2 + (target & 15) + lax.shift_right_logical(target & 128, 3)
    reorder = (source == wanted).astype(F32).astype(BF16)

    def embedding_projection(tower):
        loads[tower][5].wait()
        loads[tower][6].wait()
        total = v.skip[tower].astype(F32) + scatter_end(v.down, tower, 0)
        columns = total.astype(BF16)
        rows = columns.T

        for f in range(6):
            product = jnp.dot(
                rows, v.m[tower, :, f * 256 : f * 256 + 256], preferred_element_type=F32
            )
            product = product.reshape(8, 32, 256).astype(BF16)
            cut = min(max(640 - f * 256, 0), 256)
            if cut > 0:
                v.emb.one[tower, :, :, f * 256 : f * 256 + cut] = product[:, :, :cut]
            if cut < 256:
                start = f * 256 + cut - 640
                v.emb.other[tower, :, :, start : start + 256 - cut] = product[:, :, cut:]

        scatter_start(v.emb, tower)
        v.stream[0, tower] = jnp.dot(columns, reorder, preferred_element_type=F32).astype(BF16)

    def await_all(copies):
        for copy in copies:
            copy.wait_recv()

    def stream_step(step):
        if step < 4:
            ways = ((1, (step - 1,), (step,), step), (-1, ((9 - step) % 8,), (8 - step,), 8 - step))
        else:
            ways = ((1, (3, 0), (4, 0), 4), (-1, (5, 1), (4, 1), 8))
        return [
            send(
                v.stream.at[at], v.stream.at[to], v.stream_sem.at[0, j], v.stream_sem.at[1, j], to_z(way)
            )
            for way, at, to, j in ways
        ]

    first, second = 1, 0
    down_projection(first)
    down_projection(second)
    scatter_relay(v.down, first)
    scatter_along(v.down, first)
    scatter_relay(v.down, second)
    scatter_wide(v.down, first)
    scatter_along(v.down, second)
    scatter_wide(v.down, second)
    embedding_projection(first)
    embedding_projection(second)
    stream_ring = stream_step(1)
    scatter_relay(v.emb, first)
    scatter_along(v.emb, first)
    scatter_relay(v.emb, second)
    scatter_wide(v.emb, first)
    scatter_along(v.emb, second)
    scatter_wide(v.emb, second)
    await_all(stream_ring)
    stream_ring = stream_step(2)

    def embed(tower):
        raw = scatter_end(v.emb, tower, 1)
        norm = jnp.sqrt(jnp.sum(raw * raw, axis=1, keepdims=True) + 1e-06)
        unit = raw / norm
        v.unit[tower] = unit
        v.norm[tower] = jnp.broadcast_to(norm, (32, 128))
        return unit.astype(BF16)

    mark = len(sends)
    v.txt[0, 0] = embed(1)
    pair_copies = []
    txt_copies = {}

    def share(slot):
        pair_copies.append(
            send(v.txt.at[0, slot], v.txt.at[1, slot], v.pair_sem.at[0, slot], v.pair_sem.at[1, slot], sibling)
        )

    def txt_step(step):
        up, down = (step - 1, step, 1), ((9 - step) % 8, 8 - step, -1)
        for (at, to, way), half in ((up, 0), (down, 1), (up, 1), (down, 0)):
            if at != 0:
                txt_copies[at, half].wait_recv()
            if to != 4 or half == (way < 0):
                rows = pl.ds(half * 16, 16)
                txt_copies[to, half] = send(
                    v.txt.at[0, at, rows],
                    v.txt.at[0, to, rows],
                    v.txt_sem.at[0, to, half],
                    v.txt_sem.at[1, to, half],
                    to_z(way),
                )
        for at in {up[0], down[0]}:
            share(at)

    txt_step(1)

    unit = embed(0)
    v.img[0, 0, 0] = unit[:16]
    v.img[1, 0, 0] = unit[16:]
    ways = (to_x, to_y)

    def image_push(at, to, phase, half, k, way):
        sem = v.img_sem
        return send(
            v.img.at[at], v.img.at[to], sem.at[0, phase, half, k], sem.at[1, phase, half, k], way(k)
        )

    img_first, img_copies = ([], []), {1: [], 2: [], 3: []}
    for k in (2, 1, 3):
        for half in range(2):
            img_first[half].append(image_push((half, 0, 0), (half, 0, k), 0, half, k, ways[half]))
    for k in (2, 1, 3):
        for half in range(2):
            img_copies[k].append(image_push((half, 0, 0), (half, k, 0), 1, half, k, ways[1 - half]))

    txt_step(2)
    txt_step(3)
    turned = pl.ds(1, 3)
    for half in range(2):
        await_all(img_first[half])
        for k in (2, 1, 3):
            img_copies[k].append(
                image_push((half, 0, turned), (half, k, turned), 2, half, k, ways[1 - half])
            )
    txt_step(4)
    settle(mark)
    await_all(txt_copies[4, half] for half in range(2))
    share(4)
    await_all(stream_ring)
    stream_ring = stream_step(3)
    mark = len(sends)

    scale, shift = scale_ref[0], shift_ref[0]
    row_id = lax.broadcasted_iota(jnp.int32, (256, 256), 0)
    col_id = lax.broadcasted_iota(jnp.int32, (256, 256), 1)

    own_pair = ((row_id < 16) & (col_id == row_id)) | (
        (row_id >= 128) & (row_id < 144) & (col_id == row_id - 112)
    )

    def pair_coefficients(core, group):
        inner = lax.dot_general(
            v.img[:, 2 * group : 2 * group + 2].reshape(256, 1536),
            v.txt[core].reshape(256, 1536),
            (((1,), (1,)), ((), ())),
            preferred_element_type=F32,
        )
        value = jax.nn.sigmoid(scale * inner + shift)
        if core == 0 and group == 0:
            value = value - own_pair.astype(F32)
        value = scale * value
        turned_value = value.T.astype(BF16)
        value = value.astype(BF16)
        for half in range(2):
            part = slice(half * 128, half * 128 + 128)
            start = group * 128
            v.coef[half, start : start + 128, core * 256 : core * 256 + 256] = value[part]
            v.coef_t[core, :, half * 256 + start : half * 256 + start + 128] = turned_value[:, part]

    await_all(img_copies[1] + img_copies[2] + img_copies[3])
    pair_coefficients(0, 0)
    pair_coefficients(0, 1)
    await_all(pair_copies)
    pair_coefficients(1, 0)
    pair_coefficients(1, 1)

    def text_partials(core):
        @pl.loop(0, 6, unroll=True)
        def _(f):
            cols = pl.ds(pl.multiple_of(f * 256, 256), 256)
            product = jnp.dot(
                v.coef_t[core], v.img[:, :, :, :, cols].reshape(512, 256), preferred_element_type=F32
            ).reshape(8, 32, 256)
            if core == 0:
                v.gt_own[:, :, cols] = product
            else:
                v.gt_out[:, :, cols] = product.astype(BF16)

    def image_partials(half):
        @pl.loop(0, 6, unroll=True)
        def _(f):
            cols = pl.ds(pl.multiple_of(f * 256, 256), 256)
            product = jnp.dot(
                v.coef[half], v.txt[:, :, :, cols].reshape(512, 256), preferred_element_type=F32
            )
            v.gi_out[half, :, :, :, cols] = product.reshape(4, 4, 16, 256).astype(BF16)

    gi_first, gi_copies = ([], []), ([], [])

    def image_start(half):
        image_partials(half)
        for phase, blocks, copies in ((0, turned, gi_first), (2, pl.ds(0, 1), gi_copies)):
            for k in (2, 1, 3):
                copies[half].append(
                    send(
                        v.gi_out.at[half, k, blocks],
                        v.gi_in.at[half, k, blocks],
                        v.gi_sem.at[0, phase, half, k],
                        v.gi_sem.at[1, phase, half, k],
                        ways[1 - half](-k),
                    )
                )

    gh_copies = ([], [])

    def image_own(half, k):
        total = v.gi_out[half, 0, k].astype(F32)
        for j in range(1, 4):
            total += v.gi_in[half, j, k].astype(F32)
        return total

    def image_middle(half):
        await_all(gi_first[half])
        for k in (2, 1, 3):
            v.gh_out[half, k] = image_own(half, k).astype(BF16)
            gh_copies[half].append(
                send(
                    v.gh_out.at[half, k],
                    v.gh_in.at[half, k],
                    v.gi_sem.at[0, 1, half, k],
                    v.gi_sem.at[1, 1, half, k],
                    ways[half](-k),
                )
            )

    def image_end(half):
        await_all(gi_copies[half])
        total = image_own(half, 0)
        await_all(gh_copies[half])
        for k in range(1, 4):
            total += v.gh_in[half, k].astype(F32)
        return total

    gz_copies = {}

    def text_own(r, half):
        rows = slice(half * 16, half * 16 + 16)
        return v.gt_own[r, rows] + v.gt_in[r, rows].astype(F32)

    def text_step(step):
        moves = [(5 - step, 0, -1), (3 + step, 1, 1)]
        if step < 4:
            moves += [(4 - step, 1, -1), (4 + step, 0, 1)]
        for r, half, way in moves:
            rows = slice(half * 16, half * 16 + 16)
            total = text_own(r, half)
            before = r - way
            if (before, half) in gz_copies and (before != 4 or half == (way > 0)):
                gz_copies[before, half].wait_recv()
                total += v.gz_in[before, rows].astype(F32)
            v.gz_out[r, rows] = total.astype(BF16)
            gz_copies[r, half] = send(
                v.gz_out.at[r, pl.ds(half * 16, 16)],
                v.gz_in.at[r, pl.ds(half * 16, 16)],
                v.gz_sem.at[0, r, half],
                v.gz_sem.at[1, r, half],
                to_z(way),
            )

    def text_end(half):
        rows = slice(half * 16, half * 16 + 16)
        total = text_own(0, half)
        for r in (1, 7):
            gz_copies[r, half].wait_recv()
            total += v.gz_in[r, rows].astype(F32)
        return total

    text_partials(1)
    gt_copies = []
    for j, (start, count) in enumerate(((3, 3), (0, 3), (6, 2))):
        part = pl.ds(start, count)
        gt_copies.append(
            send(v.gt_out.at[part], v.gt_in.at[part], v.gt_sem.at[0, j], v.gt_sem.at[1, j], sibling)
        )
    text_partials(0)
    image_start(0)
    gt_copies[0].wait_recv()
    text_step(1)
    image_start(1)
    await_all(gt_copies[1:])
    settle(mark)
    text_step(2)
    text_step(3)
    image_middle(0)
    image_middle(1)
    text_step(4)
    mark = len(sends)

    turn_copies = ({}, {})

    def turn(tower, grad):
        raw = raw_gradient(grad, v.unit[tower], v.norm[tower][:, :1])
        for k in range(8):
            cols = slice(k * 192, k * 192 + 192)
            v.pack[tower, k] = jnp.concatenate([raw[:16, cols], raw[16:, cols]], axis=1)
        v.graw[tower, t, 0] = v.pack[tower, z]
        for k in (4, 3, 5, 2, 6, 1, 7):
            turn_copies[tower][k] = send(
                v.pack.at[tower, (z + k) % 8],
                v.graw.at[tower, t, k],
                v.turn_sem.at[0, tower, k],
                v.turn_sem.at[1, tower, k],
                to_z(k),
            )

    turn(1, jnp.concatenate([text_end(half) for half in range(2)], axis=0))
    turn(0, jnp.concatenate([image_end(half) for half in range(2)], axis=0))

    spread_copies, low_copies, high_copies = ([], []), {}, {}

    low_slots, high_slots = pl.ds(0, 3), pl.ds(3, 5)

    def spread(tower, owner, slots, phase, j, peer):
        block = v.graw.at[tower, owner, slots]
        sem = v.spread_sem
        return send(block, block, sem.at[0, tower, phase, j], sem.at[1, tower, phase, j], peer)

    def spread_start(tower):
        await_all(turn_copies[tower][k] for k in (1, 2))
        low_copies[tower] = spread(tower, t, low_slots, 0, 0, partner)
        await_all(turn_copies[tower][k] for k in range(3, 8))
        high_copies[tower] = {
            k: spread(tower, t, high_slots, 0, k, to_y(k)) for k in (2, 1, 3)
        }
        spread_copies[tower].append(spread(tower, t, high_slots, 1, 0, partner))
        spread_copies[tower].extend(
            spread(tower, t, low_slots, 1, k, to_y(k)) for k in (2, 1, 3)
        )

    def spread_end(tower):
        low_copies[tower].wait_recv()
        for k in (2, 1, 3):
            spread_copies[tower].append(
                spread(tower, (t + 4) % 8, low_slots, 2, k, to_y(k))
            )
        for k in (1, 3, 2):
            high_copies[tower][k].wait_recv()
            owner = low * 4 + (y - k) % 4
            spread_copies[tower].append(spread(tower, owner, high_slots, 2, k + 4, partner))

    def contract(tower):
        await_all(spread_copies[tower])
        totals = [jnp.zeros((192, 256), F32)] * 2
        for r in range(0, 8, 2):
            rows = jnp.concatenate([v.graw[tower, :, r + i].reshape(128, 384) for i in range(2)], axis=0)
            for half in range(2):
                lanes = slice(half * 128, half * 128 + 128)
                columns = jnp.concatenate([v.stream[r + i, tower, :, lanes] for i in range(2)], axis=1)
                totals[half] += jnp.dot(
                    columns, rows[:, half * 128 : half * 128 + 256], preferred_element_type=F32
                )
        total = totals[0][:, :192] + totals[1][:, 64:]
        return jnp.concatenate([total, jnp.zeros((64, 192), F32)], axis=0).T

    await_all(stream_ring)
    stream_ring = stream_step(4)
    spread_start(first)
    spread_start(second)
    settle(mark)
    spread_end(first)
    spread_end(second)
    mark = len(sends)
    await_all(stream_ring)

    part_copies = ([], [])
    for tower in (first, second):
        columns = contract(tower)
        for q in range(4):
            v.part[tower, q] = columns[q * 48 : q * 48 + 48]
        for k in (3, 2, 1):
            x_to, c_to = (x + k // 2 * 2) % 4, (c + k) % 2
            part_copies[tower].append(
                send(
                    v.part.at[tower, x_to // 2 * 2 + c_to],
                    v.part_in.at[tower, k],
                    v.part_sem.at[0, tower, k],
                    v.part_sem.at[1, tower, k],
                    device(z, x_to, y, c_to),
                )
            )
    settle(mark)
    totals = {}
    for tower in (first, second):
        total = v.part[tower, d % 4]
        for k in (1, 2, 3):
            part_copies[tower][3 - k].wait_recv()
            total += v.part_in[tower, k]
        totals[tower] = total[:, :192]
    output[...] = jnp.concatenate([totals[0], totals[1]], axis=1)
    settle(len(sends))


def on_device(
    picture_skip_entries,
    picture_activations,
    picture_contract_weights,
    picture_embedding_map,
    caption_skip_entries,
    caption_activations,
    caption_contract_weights,
    caption_embedding_map,
    sharpness_coefficient,
    pairwise_score_shift,
):
    both = pl.pallas_call(
        window_kernel,
        out_shape=jax.ShapeDtypeStruct((48, 384), F32),
        in_specs=[pl.BlockSpec(memory_space=pl.ANY)] * 8
        + [pl.BlockSpec(memory_space=pltpu.SMEM)] * 2,
        out_specs=pl.BlockSpec(memory_space=pltpu.VMEM),
        scratch_shapes=[*SCRATCH.values(), *DOWN.values(), *EMB.values()],
        compiler_params=pltpu.CompilerParams(
            collective_id=0, has_side_effects=True, vmem_limit_bytes=VMEM_LIMIT
        ),
    )(
        picture_activations,
        picture_contract_weights,
        picture_embedding_map,
        picture_skip_entries.T,
        caption_activations,
        caption_contract_weights,
        caption_embedding_map,
        caption_skip_entries.T,
        sharpness_coefficient,
        pairwise_score_shift,
    )
    return both[:, :192].T, both[:, 192:].T


def solution(mesh):
    placed = (
        P("dp", "tensor"),
        P("dp", "tensor"),
        P("tensor", None),
        P("tensor", None),
        P("dp", "tensor"),
        P("dp", "tensor"),
        P("tensor", None),
        P("tensor", None),
        P(),
        P(),
    )
    return jax.shard_map(
        on_device,
        mesh=mesh,
        in_specs=placed,
        out_specs=(P("tensor", "dp"), P("tensor", "dp")),
        check_vma=False,
    )
```

```python
from types import SimpleNamespace

import jax
import jax.numpy as jnp
from jax import lax
from jax.experimental import pallas as pl
from jax.experimental.pallas import tpu as pltpu
from jax.sharding import PartitionSpec as P

MESH = pl.DeviceIdType.MESH
BF16, F32 = jnp.bfloat16, jnp.float32
VMEM_LIMIT = 60 * 1024 * 1024


def device(z, x, y, c):
    return (z * 4 + x // 2 * 2 + c, x % 2 * 4 + y)


def push(src, dst, send, recv, peer):
    copy = pltpu.make_async_remote_copy(
        src_ref=src, dst_ref=dst, send_sem=send, recv_sem=recv, device_id=peer, device_id_type=MESH
    )
    copy.start()
    return copy


def raw_gradient(grad, unit, norm):
    along = jnp.sum(unit * grad, axis=1, keepdims=True)
    return ((grad - unit * along) / norm).astype(BF16)


def scatter_scratch(one, other):
    return dict(
        one=pltpu.VMEM((2, 8, *one), BF16),
        other=pltpu.VMEM((2, 8, *other), BF16),
        cross_in=pltpu.VMEM((2, 4, *one), BF16),
        half_out=pltpu.VMEM((2, 4, *one), BF16),
        half_in=pltpu.VMEM((2, 4, *one), BF16),
        round_out=pltpu.VMEM((2, 2, *other), BF16),
        round_in=pltpu.VMEM((2, 6, *other), BF16),
        wide_out=pltpu.VMEM((2, 2, *other), BF16),
        wide_in=pltpu.VMEM((2, *other), BF16),
        sem=pltpu.SemaphoreType.DMA((2, 2, 12)),
    )


DOWN = scatter_scratch((80, 256), (112, 256))
EMB = scatter_scratch((32, 640), (32, 896))
SCRATCH = dict(
    act=pltpu.VMEM((2, 256, 768), BF16),
    w=pltpu.VMEM((2, 768, 1536), BF16),
    m=pltpu.VMEM((2, 192, 1536), BF16),
    skip=pltpu.VMEM((2, 192, 256), BF16),
    stream=pltpu.VMEM((8, 2, 192, 256), BF16),
    unit=pltpu.VMEM((2, 32, 1536), F32),
    norm=pltpu.VMEM((2, 32, 128), F32),
    img=pltpu.VMEM((2, 4, 4, 16, 1536), BF16),
    txt=pltpu.VMEM((2, 8, 32, 1536), BF16),
    coef=pltpu.VMEM((2, 256, 512), BF16),
    coef_t=pltpu.VMEM((2, 256, 512), BF16),
    gt_own=pltpu.VMEM((8, 32, 1536), F32),
    gt_out=pltpu.VMEM((8, 32, 1536), BF16),
    gt_in=pltpu.VMEM((8, 32, 1536), BF16),
    gz_out=pltpu.VMEM((8, 32, 1536), BF16),
    gz_in=pltpu.VMEM((8, 32, 1536), BF16),
    gi_out=pltpu.VMEM((2, 4, 4, 16, 1536), BF16),
    gi_in=pltpu.VMEM((2, 4, 4, 16, 1536), BF16),
    gh_out=pltpu.VMEM((2, 4, 16, 1536), BF16),
    gh_in=pltpu.VMEM((2, 4, 16, 1536), BF16),
    pack=pltpu.VMEM((2, 8, 16, 384), BF16),
    graw=pltpu.VMEM((2, 8, 8, 16, 384), BF16),
    part=pltpu.VMEM((2, 4, 48, 256), F32),
    part_in=pltpu.VMEM((2, 4, 48, 256), F32),
    load_sem=pltpu.SemaphoreType.DMA((2, 7)),
    stream_sem=pltpu.SemaphoreType.DMA((2, 8, 2)),
    img_sem=pltpu.SemaphoreType.DMA((2, 3, 2, 4)),
    txt_sem=pltpu.SemaphoreType.DMA((2, 8, 2)),
    pair_sem=pltpu.SemaphoreType.DMA((2, 8)),
    gt_sem=pltpu.SemaphoreType.DMA((2, 3)),
    gz_sem=pltpu.SemaphoreType.DMA((2, 8, 2)),
    gi_sem=pltpu.SemaphoreType.DMA((2, 3, 2, 4)),
    turn_sem=pltpu.SemaphoreType.DMA((2, 2, 8)),
    spread_sem=pltpu.SemaphoreType.DMA((2, 2, 3, 8)),
    part_sem=pltpu.SemaphoreType.DMA((2, 2, 4)),
)


def window_kernel(*refs):
    inputs, (scale_ref, shift_ref), output = refs[:8], refs[8:10], refs[10]
    count = len(SCRATCH)
    v = SimpleNamespace(**dict(zip(SCRATCH, refs[11:])))
    v.down = SimpleNamespace(**dict(zip(DOWN, refs[11 + count :])))
    v.emb = SimpleNamespace(**dict(zip(EMB, refs[11 + count + len(DOWN) :])))
    for s in (v.down, v.emb):
        s.relay, s.cross, s.near, s.last, s.along, s.wide = ({} for _ in range(6))
    d, t = lax.axis_index("dp"), lax.axis_index("tensor")
    z, x, y, c = d // 4, d // 2 % 2 * 2 + t // 4, t % 4, d % 2
    sends, settled = [], [0]

    def send(*args):
        copy = push(*args)
        sends.append(copy)
        return copy

    def settle(mark):
        for copy in sends[settled[0] : mark]:
            copy.wait_send()
        settled[0] = max(settled[0], mark)

    def to_x(k):
        return device(z, (x + k) % 4, y, c)

    def to_y(k):
        return (d, t // 4 * 4 + (y + k) % 4)

    def to_z(k):
        return ((z + k) % 8 * 4 + d % 4, t)

    sibling = (d // 2 * 2 + 1 - c, t)

    loads = {}
    for tower in (1, 0):
        act, w, m, skip = inputs[tower * 4 : tower * 4 + 4]
        pairs = [(act, v.act.at[tower])]
        for f in range(4):
            cols = pl.ds(f * 384, 384)
            pairs.append((w.at[:, cols], v.w.at[tower, :, cols]))
        pairs += [(m, v.m.at[tower]), (skip, v.skip.at[tower])]
        row = []
        for j, (source, target) in enumerate(pairs):
            load = pltpu.make_async_copy(source, target, v.load_sem.at[tower, j])
            load.start()
            row.append(load)
        loads[tower] = row

    peers = [(d, (t + k) % 8) for k in range(1, 8)]
    peers += [to_z(k) for k in range(1, 8)]
    peers += [device(z, (x + 2) % 4, y, c), device(z, (x // 2 * 2 + 2) % 4 + 1 - x % 2, y, c)]
    peers += [sibling, device(z, (x + 2) % 4, y, 1 - c)]
    barrier = pltpu.get_barrier_semaphore()
    for peer in peers:
        pl.semaphore_signal(barrier, inc=1, device_id=peer, device_id_type=MESH)

    low = t // 4
    partner = (d, (t + 4) % 8)

    def scatter_start(s, tower):
        def hop(j, k, wide, way):
            return send(
                s.other.at[tower, wide * 4 + (y + k) % 4],
                s.round_in.at[tower, j],
                s.sem.at[0, tower, j],
                s.sem.at[1, tower, j],
                to_y(way),
            )

        s.relay[tower] = [hop(0, 2, 0, 1), hop(1, 2, 1, -1)]
        s.cross[tower] = send(
            s.one.at[tower, pl.ds((1 - low) * 4, 4)],
            s.cross_in.at[tower],
            s.sem.at[0, tower, 6],
            s.sem.at[1, tower, 6],
            partner,
        )
        s.near[tower] = [hop(2, 1, 1, 1), hop(3, 3, 0, -1)]

    def half_sum(s, tower, k):
        place = (y + k) % 4
        return s.one[tower, low * 4 + place].astype(F32) + s.cross_in[tower, place].astype(F32)

    def scatter_relay(s, tower):
        s.last[tower] = []
        for j, way in ((0, 1), (1, -1)):
            s.relay[tower][j].wait_recv()
            total = s.other[tower, j * 4 + (y + way) % 4].astype(F32)
            total += s.round_in[tower, j].astype(F32)
            s.round_out[tower, j] = total.astype(BF16)
            s.last[tower].append(
                send(
                    s.round_out.at[tower, j],
                    s.round_in.at[tower, 4 + j],
                    s.sem.at[0, tower, 4 + j],
                    s.sem.at[1, tower, 4 + j],
                    to_y(way),
                )
            )

    def scatter_along(s, tower):
        s.cross[tower].wait_recv()
        s.along[tower] = []
        for k in (2, 1, 3):
            s.half_out[tower, k] = half_sum(s, tower, k).astype(BF16)
            s.along[tower].append(
                send(
                    s.half_out.at[tower, k],
                    s.half_in.at[tower, k],
                    s.sem.at[0, tower, 7 + k],
                    s.sem.at[1, tower, 7 + k],
                    to_y(k),
                )
            )

    def scatter_wide(s, tower):
        for j in range(2):
            s.near[tower][1 - j].wait_recv()
            s.last[tower][j].wait_recv()
            total = s.other[tower, j * 4 + y].astype(F32)
            total += s.round_in[tower, 3 - j].astype(F32)
            total += s.round_in[tower, 4 + j].astype(F32)
            s.wide_out[tower, j] = total.astype(BF16)
        s.wide[tower] = send(
            s.wide_out.at[tower, 1 - low],
            s.wide_in.at[tower],
            s.sem.at[0, tower, 11],
            s.sem.at[1, tower, 11],
            partner,
        )

    def scatter_end(s, tower, axis):
        first = half_sum(s, tower, 0)
        for k in (1, 3, 2):
            s.along[tower][(2, 1, 3).index(k)].wait_recv()
            first += s.half_in[tower, k].astype(F32)
        s.wide[tower].wait_recv()
        second = s.wide_out[tower, low].astype(F32) + s.wide_in[tower].astype(F32)
        return jnp.concatenate([first, second], axis=axis)

    def down_projection(tower):
        loads[tower][0].wait()
        for f in range(4):
            loads[tower][1 + f].wait()
            product = jnp.dot(
                v.act[tower], v.w[tower, :, f * 384 : f * 384 + 384], preferred_element_type=F32
            )
            product = product.T.reshape(2, 192, 256).astype(BF16)
            v.down.one[tower, 2 * f : 2 * f + 2] = product[:, :80]
            v.down.other[tower, 2 * f : 2 * f + 2] = product[:, 80:]

        if tower == 1:
            pl.semaphore_wait(barrier, len(peers))
        scatter_start(v.down, tower)

    source = lax.broadcasted_iota(jnp.int32, (256, 256), 0)
    target = lax.broadcasted_iota(jnp.int32, (256, 256), 1)
    wanted = (target & 112) * 2 + (target & 15) + lax.shift_right_logical(target & 128, 3)
    reorder = (source == wanted).astype(F32).astype(BF16)

    def embedding_projection(tower):
        loads[tower][5].wait()
        loads[tower][6].wait()
        total = v.skip[tower].astype(F32) + scatter_end(v.down, tower, 0)
        columns = total.astype(BF16)
        rows = columns.T

        for f in range(6):
            product = jnp.dot(
                rows, v.m[tower, :, f * 256 : f * 256 + 256], preferred_element_type=F32
            )
            product = product.reshape(8, 32, 256).astype(BF16)
            cut = min(max(640 - f * 256, 0), 256)
            if cut > 0:
                v.emb.one[tower, :, :, f * 256 : f * 256 + cut] = product[:, :, :cut]
            if cut < 256:
                start = f * 256 + cut - 640
                v.emb.other[tower, :, :, start : start + 256 - cut] = product[:, :, cut:]

        scatter_start(v.emb, tower)
        v.stream[0, tower] = jnp.dot(columns, reorder, preferred_element_type=F32).astype(BF16)

    def await_all(copies):
        for copy in copies:
            copy.wait_recv()

    def stream_push(at, to, tower, way):
        sem = v.stream_sem
        return send(
            v.stream.at[at, tower],
            v.stream.at[to, tower],
            sem.at[0, to, tower],
            sem.at[1, to, tower],
            to_z(way),
        )

    def stream_step(step, tower):
        if step < 4:
            up = stream_push(step - 1, step, tower, 1)
            return [up, stream_push((9 - step) % 8, 8 - step, tower, -1)]
        return [stream_push(3, 4, 0, 1) if tower == 0 else stream_push(5, 4, 1, -1)]

    first, second = 1, 0
    down_projection(first)
    down_projection(second)
    scatter_relay(v.down, first)
    scatter_along(v.down, first)
    scatter_relay(v.down, second)
    scatter_wide(v.down, first)
    scatter_along(v.down, second)
    scatter_wide(v.down, second)
    stream_ring = {}
    embedding_projection(first)
    stream_ring[first] = stream_step(1, first)
    embedding_projection(second)
    stream_ring[second] = stream_step(1, second)

    def stream_next(step, tower):
        await_all(stream_ring[tower])
        stream_ring[tower] = stream_step(step, tower)

    scatter_relay(v.emb, first)
    scatter_along(v.emb, first)
    scatter_relay(v.emb, second)
    stream_next(2, first)
    scatter_wide(v.emb, first)
    stream_next(2, second)
    scatter_along(v.emb, second)
    scatter_wide(v.emb, second)

    def embed(tower):
        raw = scatter_end(v.emb, tower, 1)
        norm = jnp.sqrt(jnp.sum(raw * raw, axis=1, keepdims=True) + 1e-06)
        unit = raw / norm
        v.unit[tower] = unit
        v.norm[tower] = jnp.broadcast_to(norm, (32, 128))
        return unit.astype(BF16)

    mark = len(sends)
    v.txt[0, 0] = embed(1)
    pair_copies = []
    txt_copies = {}

    def share(slot):
        pair_copies.append(
            send(v.txt.at[0, slot], v.txt.at[1, slot], v.pair_sem.at[0, slot], v.pair_sem.at[1, slot], sibling)
        )

    def txt_step(step):
        up, down = (step - 1, step, 1), ((9 - step) % 8, 8 - step, -1)
        for (at, to, way), half in ((up, 0), (down, 1), (up, 1), (down, 0)):
            if at != 0:
                txt_copies[at, half].wait_recv()
            if to != 4 or half == (way < 0):
                rows = pl.ds(half * 16, 16)
                txt_copies[to, half] = send(
                    v.txt.at[0, at, rows],
                    v.txt.at[0, to, rows],
                    v.txt_sem.at[0, to, half],
                    v.txt_sem.at[1, to, half],
                    to_z(way),
                )
        for at in {up[0], down[0]}:
            share(at)

    txt_step(1)

    unit = embed(0)
    v.img[0, 0, 0] = unit[:16]
    v.img[1, 0, 0] = unit[16:]
    ways = (to_x, to_y)

    def image_push(at, to, phase, half, k, way):
        sem = v.img_sem
        return send(
            v.img.at[at], v.img.at[to], sem.at[0, phase, half, k], sem.at[1, phase, half, k], way(k)
        )

    img_first, img_copies = ([], []), {1: [], 2: [], 3: []}
    for k in (2, 1, 3):
        for half in range(2):
            img_first[half].append(image_push((half, 0, 0), (half, 0, k), 0, half, k, ways[half]))
    for k in (2, 1, 3):
        for half in range(2):
            img_copies[k].append(image_push((half, 0, 0), (half, k, 0), 1, half, k, ways[1 - half]))

    txt_step(2)
    txt_step(3)
    turned = pl.ds(1, 3)
    for half in range(2):
        await_all(img_first[half])
        for k in (2, 1, 3):
            img_copies[k].append(
                image_push((half, 0, turned), (half, k, turned), 2, half, k, ways[1 - half])
            )
    txt_step(4)
    settle(mark)
    await_all(txt_copies[4, half] for half in range(2))
    share(4)
    stream_next(3, first)
    stream_next(3, second)
    mark = len(sends)

    scale, shift = scale_ref[0], shift_ref[0]
    row_id = lax.broadcasted_iota(jnp.int32, (256, 256), 0)
    col_id = lax.broadcasted_iota(jnp.int32, (256, 256), 1)

    own_pair = ((row_id < 16) & (col_id == row_id)) | (
        (row_id >= 128) & (row_id < 144) & (col_id == row_id - 112)
    )

    def pair_coefficients(core, group):
        inner = lax.dot_general(
            v.img[:, 2 * group : 2 * group + 2].reshape(256, 1536),
            v.txt[core].reshape(256, 1536),
            (((1,), (1,)), ((), ())),
            preferred_element_type=F32,
        )
        value = jax.nn.sigmoid(scale * inner + shift)
        if core == 0 and group == 0:
            value = value - own_pair.astype(F32)
        value = scale * value
        turned_value = value.T.astype(BF16)
        value = value.astype(BF16)
        for half in range(2):
            part = slice(half * 128, half * 128 + 128)
            start = group * 128
            v.coef[half, start : start + 128, core * 256 : core * 256 + 256] = value[part]
            v.coef_t[core, :, half * 256 + start : half * 256 + start + 128] = turned_value[:, part]

    await_all(img_copies[1] + img_copies[2] + img_copies[3])
    pair_coefficients(0, 0)
    pair_coefficients(0, 1)
    await_all(pair_copies)
    pair_coefficients(1, 0)
    pair_coefficients(1, 1)

    def text_partials(core):
        @pl.loop(0, 6, unroll=True)
        def _(f):
            cols = pl.ds(pl.multiple_of(f * 256, 256), 256)
            product = jnp.dot(
                v.coef_t[core], v.img[:, :, :, :, cols].reshape(512, 256), preferred_element_type=F32
            ).reshape(8, 32, 256)
            if core == 0:
                v.gt_own[:, :, cols] = product
            else:
                v.gt_out[:, :, cols] = product.astype(BF16)

    def image_partials(half):
        @pl.loop(0, 6, unroll=True)
        def _(f):
            cols = pl.ds(pl.multiple_of(f * 256, 256), 256)
            product = jnp.dot(
                v.coef[half], v.txt[:, :, :, cols].reshape(512, 256), preferred_element_type=F32
            )
            v.gi_out[half, :, :, :, cols] = product.reshape(4, 4, 16, 256).astype(BF16)

    gi_first, gi_copies = ([], []), ([], [])

    def image_start(half):
        image_partials(half)
        for phase, blocks, copies in ((0, turned, gi_first), (2, pl.ds(0, 1), gi_copies)):
            for k in (2, 1, 3):
                copies[half].append(
                    send(
                        v.gi_out.at[half, k, blocks],
                        v.gi_in.at[half, k, blocks],
                        v.gi_sem.at[0, phase, half, k],
                        v.gi_sem.at[1, phase, half, k],
                        ways[1 - half](-k),
                    )
                )

    gh_copies = ([], [])

    def image_own(half, k):
        total = v.gi_out[half, 0, k].astype(F32)
        for j in range(1, 4):
            total += v.gi_in[half, j, k].astype(F32)
        return total

    def image_middle(half):
        await_all(gi_first[half])
        for k in (2, 1, 3):
            v.gh_out[half, k] = image_own(half, k).astype(BF16)
            gh_copies[half].append(
                send(
                    v.gh_out.at[half, k],
                    v.gh_in.at[half, k],
                    v.gi_sem.at[0, 1, half, k],
                    v.gi_sem.at[1, 1, half, k],
                    ways[half](-k),
                )
            )

    def image_end(half):
        await_all(gi_copies[half])
        total = image_own(half, 0)
        await_all(gh_copies[half])
        for k in range(1, 4):
            total += v.gh_in[half, k].astype(F32)
        return total

    gz_copies = {}

    def text_own(r, half):
        rows = slice(half * 16, half * 16 + 16)
        return v.gt_own[r, rows] + v.gt_in[r, rows].astype(F32)

    def text_step(step):
        moves = [(5 - step, 0, -1), (3 + step, 1, 1)]
        if step < 4:
            moves += [(4 - step, 1, -1), (4 + step, 0, 1)]
        for r, half, way in moves:
            rows = slice(half * 16, half * 16 + 16)
            total = text_own(r, half)
            before = r - way
            if (before, half) in gz_copies and (before != 4 or half == (way > 0)):
                gz_copies[before, half].wait_recv()
                total += v.gz_in[before, rows].astype(F32)
            v.gz_out[r, rows] = total.astype(BF16)
            gz_copies[r, half] = send(
                v.gz_out.at[r, pl.ds(half * 16, 16)],
                v.gz_in.at[r, pl.ds(half * 16, 16)],
                v.gz_sem.at[0, r, half],
                v.gz_sem.at[1, r, half],
                to_z(way),
            )

    def text_end(half):
        rows = slice(half * 16, half * 16 + 16)
        total = text_own(0, half)
        for r in (1, 7):
            gz_copies[r, half].wait_recv()
            total += v.gz_in[r, rows].astype(F32)
        return total

    text_partials(1)
    gt_copies = []
    for j, (start, count) in enumerate(((3, 3), (0, 3), (6, 2))):
        part = pl.ds(start, count)
        gt_copies.append(
            send(v.gt_out.at[part], v.gt_in.at[part], v.gt_sem.at[0, j], v.gt_sem.at[1, j], sibling)
        )
    text_partials(0)
    image_start(0)
    gt_copies[0].wait_recv()
    text_step(1)
    image_start(1)
    await_all(gt_copies[1:])
    settle(mark)
    text_step(2)
    text_step(3)
    image_middle(0)
    image_middle(1)
    text_step(4)
    mark = len(sends)

    turn_copies = ({}, {})

    def turn(tower, grad):
        raw = raw_gradient(grad, v.unit[tower], v.norm[tower][:, :1])
        for k in range(8):
            cols = slice(k * 192, k * 192 + 192)
            v.pack[tower, k] = jnp.concatenate([raw[:16, cols], raw[16:, cols]], axis=1)
        v.graw[tower, t, 0] = v.pack[tower, z]
        for k in (4, 3, 5, 2, 6, 1, 7):
            turn_copies[tower][k] = send(
                v.pack.at[tower, (z + k) % 8],
                v.graw.at[tower, t, k],
                v.turn_sem.at[0, tower, k],
                v.turn_sem.at[1, tower, k],
                to_z(k),
            )

    turn(1, jnp.concatenate([text_end(half) for half in range(2)], axis=0))
    turn(0, jnp.concatenate([image_end(half) for half in range(2)], axis=0))

    spread_copies, low_copies, high_copies = ([], []), {}, {}

    low_slots, high_slots = pl.ds(0, 3), pl.ds(3, 5)

    def spread(tower, owner, slots, phase, j, peer):
        block = v.graw.at[tower, owner, slots]
        sem = v.spread_sem
        return send(block, block, sem.at[0, tower, phase, j], sem.at[1, tower, phase, j], peer)

    def spread_start(tower):
        await_all(turn_copies[tower][k] for k in (1, 2))
        low_copies[tower] = spread(tower, t, low_slots, 0, 0, partner)
        await_all(turn_copies[tower][k] for k in range(3, 8))
        high_copies[tower] = {
            k: spread(tower, t, high_slots, 0, k, to_y(k)) for k in (2, 1, 3)
        }
        spread_copies[tower].append(spread(tower, t, high_slots, 1, 0, partner))
        spread_copies[tower].extend(
            spread(tower, t, low_slots, 1, k, to_y(k)) for k in (2, 1, 3)
        )

    def spread_end(tower):
        low_copies[tower].wait_recv()
        for k in (2, 1, 3):
            spread_copies[tower].append(
                spread(tower, (t + 4) % 8, low_slots, 2, k, to_y(k))
            )
        for k in (1, 3, 2):
            high_copies[tower][k].wait_recv()
            owner = low * 4 + (y - k) % 4
            spread_copies[tower].append(spread(tower, owner, high_slots, 2, k + 4, partner))

    def contract(tower):
        await_all(spread_copies[tower])
        totals = [jnp.zeros((192, 256), F32)] * 2
        for r in range(0, 8, 2):
            rows = jnp.concatenate([v.graw[tower, :, r + i].reshape(128, 384) for i in range(2)], axis=0)
            for half in range(2):
                lanes = slice(half * 128, half * 128 + 128)
                columns = jnp.concatenate([v.stream[r + i, tower, :, lanes] for i in range(2)], axis=1)
                totals[half] += jnp.dot(
                    columns, rows[:, half * 128 : half * 128 + 256], preferred_element_type=F32
                )
        total = totals[0][:, :192] + totals[1][:, 64:]
        return jnp.concatenate([total, jnp.zeros((64, 192), F32)], axis=0).T

    stream_next(4, first)
    stream_next(4, second)
    spread_start(first)
    spread_start(second)
    settle(mark)
    spread_end(first)
    spread_end(second)
    mark = len(sends)
    await_all(stream_ring[first] + stream_ring[second])

    part_copies = ([], [])
    for tower in (first, second):
        columns = contract(tower)
        for q in range(4):
            v.part[tower, q] = columns[q * 48 : q * 48 + 48]
        for k in (3, 2, 1):
            x_to, c_to = (x + k // 2 * 2) % 4, (c + k) % 2
            part_copies[tower].append(
                send(
                    v.part.at[tower, x_to // 2 * 2 + c_to],
                    v.part_in.at[tower, k],
                    v.part_sem.at[0, tower, k],
                    v.part_sem.at[1, tower, k],
                    device(z, x_to, y, c_to),
                )
            )
    settle(mark)
    totals = {}
    for tower in (first, second):
        total = v.part[tower, d % 4]
        for k in (1, 2, 3):
            part_copies[tower][3 - k].wait_recv()
            total += v.part_in[tower, k]
        totals[tower] = total[:, :192]
    output[...] = jnp.concatenate([totals[0], totals[1]], axis=1)
    settle(len(sends))


def on_device(
    picture_skip_entries,
    picture_activations,
    picture_contract_weights,
    picture_embedding_map,
    caption_skip_entries,
    caption_activations,
    caption_contract_weights,
    caption_embedding_map,
    sharpness_coefficient,
    pairwise_score_shift,
):
    both = pl.pallas_call(
        window_kernel,
        out_shape=jax.ShapeDtypeStruct((48, 384), F32),
        in_specs=[pl.BlockSpec(memory_space=pl.ANY)] * 8
        + [pl.BlockSpec(memory_space=pltpu.SMEM)] * 2,
        out_specs=pl.BlockSpec(memory_space=pltpu.VMEM),
        scratch_shapes=[*SCRATCH.values(), *DOWN.values(), *EMB.values()],
        compiler_params=pltpu.CompilerParams(
            collective_id=0, has_side_effects=True, vmem_limit_bytes=VMEM_LIMIT
        ),
    )(
        picture_activations,
        picture_contract_weights,
        picture_embedding_map,
        picture_skip_entries.T,
        caption_activations,
        caption_contract_weights,
        caption_embedding_map,
        caption_skip_entries.T,
        sharpness_coefficient,
        pairwise_score_shift,
    )
    return both[:, :192].T, both[:, 192:].T


def solution(mesh):
    placed = (
        P("dp", "tensor"),
        P("dp", "tensor"),
        P("tensor", None),
        P("tensor", None),
        P("dp", "tensor"),
        P("dp", "tensor"),
        P("tensor", None),
        P("tensor", None),
        P(),
        P(),
    )
    return jax.shard_map(
        on_device,
        mesh=mesh,
        in_specs=placed,
        out_specs=(P("tensor", "dp"), P("tensor", "dp")),
        check_vma=False,
    )
```

```python
from types import SimpleNamespace

import jax
import jax.numpy as jnp
from jax import lax
from jax.experimental import pallas as pl
from jax.experimental.pallas import tpu as pltpu
from jax.sharding import PartitionSpec as P

MESH = pl.DeviceIdType.MESH
BF16, F32 = jnp.bfloat16, jnp.float32
VMEM_LIMIT = 60 * 1024 * 1024


def device(z, x, y, c):
    return (z * 4 + x // 2 * 2 + c, x % 2 * 4 + y)


def push(src, dst, send, recv, peer):
    copy = pltpu.make_async_remote_copy(
        src_ref=src, dst_ref=dst, send_sem=send, recv_sem=recv, device_id=peer, device_id_type=MESH
    )
    copy.start()
    return copy


def raw_gradient(grad, unit, norm):
    along = jnp.sum(unit * grad, axis=1, keepdims=True)
    return ((grad - unit * along) / norm).astype(BF16)


def scatter_scratch(one, other):
    return dict(
        one=pltpu.VMEM((2, 8, *one), BF16),
        other=pltpu.VMEM((2, 8, *other), BF16),
        cross_in=pltpu.VMEM((2, 4, *one), BF16),
        half_out=pltpu.VMEM((2, 4, *one), BF16),
        half_in=pltpu.VMEM((2, 4, *one), BF16),
        round_out=pltpu.VMEM((2, 2, *other), BF16),
        round_in=pltpu.VMEM((2, 6, *other), BF16),
        wide_out=pltpu.VMEM((2, 2, *other), BF16),
        wide_in=pltpu.VMEM((2, *other), BF16),
        sem=pltpu.SemaphoreType.DMA((2, 2, 12)),
    )


DOWN = scatter_scratch((80, 256), (112, 256))
EMB = scatter_scratch((32, 640), (32, 896))
SCRATCH = dict(
    act=pltpu.VMEM((2, 256, 768), BF16),
    w=pltpu.VMEM((2, 768, 1536), BF16),
    m=pltpu.VMEM((2, 192, 1536), BF16),
    skip=pltpu.VMEM((2, 192, 256), BF16),
    stream=pltpu.VMEM((8, 2, 192, 256), BF16),
    unit=pltpu.VMEM((2, 32, 1536), F32),
    norm=pltpu.VMEM((2, 32, 128), F32),
    img=pltpu.VMEM((2, 4, 4, 16, 1536), BF16),
    txt=pltpu.VMEM((2, 8, 32, 1536), BF16),
    coef=pltpu.VMEM((2, 256, 512), BF16),
    coef_t=pltpu.VMEM((2, 256, 512), BF16),
    gt_own=pltpu.VMEM((8, 32, 1536), F32),
    gt_out=pltpu.VMEM((8, 32, 1536), BF16),
    gt_in=pltpu.VMEM((8, 32, 1536), BF16),
    gz_out=pltpu.VMEM((8, 32, 1536), BF16),
    gz_in=pltpu.VMEM((8, 32, 1536), BF16),
    gi_out=pltpu.VMEM((2, 4, 4, 16, 1536), BF16),
    gi_in=pltpu.VMEM((2, 4, 4, 16, 1536), BF16),
    gh_out=pltpu.VMEM((2, 4, 16, 1536), BF16),
    gh_in=pltpu.VMEM((2, 4, 16, 1536), BF16),
    pack=pltpu.VMEM((2, 8, 16, 384), BF16),
    graw=pltpu.VMEM((2, 8, 8, 16, 384), BF16),
    part=pltpu.VMEM((2, 2, 2, 48, 256), F32),
    part_in=pltpu.VMEM((2, 2, 48, 256), F32),
    last_out=pltpu.VMEM((2, 48, 256), F32),
    last_in=pltpu.VMEM((2, 48, 256), F32),
    load_sem=pltpu.SemaphoreType.DMA((2, 7)),
    stream_sem=pltpu.SemaphoreType.DMA((2, 8, 2)),
    img_sem=pltpu.SemaphoreType.DMA((2, 3, 2, 4)),
    txt_sem=pltpu.SemaphoreType.DMA((2, 8, 2)),
    pair_sem=pltpu.SemaphoreType.DMA((2, 8)),
    gt_sem=pltpu.SemaphoreType.DMA((2, 3)),
    gz_sem=pltpu.SemaphoreType.DMA((2, 8, 2)),
    gi_sem=pltpu.SemaphoreType.DMA((2, 3, 2, 4)),
    turn_sem=pltpu.SemaphoreType.DMA((2, 2, 8)),
    spread_sem=pltpu.SemaphoreType.DMA((2, 2, 3, 8)),
    part_sem=pltpu.SemaphoreType.DMA((2, 2, 2)),
)


def window_kernel(*refs):
    inputs, (scale_ref, shift_ref), output = refs[:8], refs[8:10], refs[10]
    count = len(SCRATCH)
    v = SimpleNamespace(**dict(zip(SCRATCH, refs[11:])))
    v.down = SimpleNamespace(**dict(zip(DOWN, refs[11 + count :])))
    v.emb = SimpleNamespace(**dict(zip(EMB, refs[11 + count + len(DOWN) :])))
    for s in (v.down, v.emb):
        s.relay, s.cross, s.near, s.last, s.along, s.wide = ({} for _ in range(6))
    d, t = lax.axis_index("dp"), lax.axis_index("tensor")
    z, x, y, c = d // 4, d // 2 % 2 * 2 + t // 4, t % 4, d % 2
    sends, settled = [], [0]

    def send(*args):
        copy = push(*args)
        sends.append(copy)
        return copy

    def settle(mark):
        for copy in sends[settled[0] : mark]:
            copy.wait_send()
        settled[0] = max(settled[0], mark)

    def to_x(k):
        return device(z, (x + k) % 4, y, c)

    def to_y(k):
        return (d, t // 4 * 4 + (y + k) % 4)

    def to_z(k):
        return ((z + k) % 8 * 4 + d % 4, t)

    sibling = (d // 2 * 2 + 1 - c, t)

    loads = {}
    for tower in (1, 0):
        act, w, m, skip = inputs[tower * 4 : tower * 4 + 4]
        pairs = [(act, v.act.at[tower])]
        for f in range(4):
            cols = pl.ds(f * 384, 384)
            pairs.append((w.at[:, cols], v.w.at[tower, :, cols]))
        pairs += [(m, v.m.at[tower]), (skip, v.skip.at[tower])]
        row = []
        for j, (source, target) in enumerate(pairs):
            load = pltpu.make_async_copy(source, target, v.load_sem.at[tower, j])
            load.start()
            row.append(load)
        loads[tower] = row

    peers = [(d, (t + k) % 8) for k in range(1, 8)]
    peers += [to_z(k) for k in range(1, 8)]
    peers += [device(z, (x + 2) % 4, y, c), device(z, (x // 2 * 2 + 2) % 4 + 1 - x % 2, y, c)]
    peers += [sibling]
    barrier = pltpu.get_barrier_semaphore()
    for peer in peers:
        pl.semaphore_signal(barrier, inc=1, device_id=peer, device_id_type=MESH)

    low = t // 4
    partner = (d, (t + 4) % 8)

    def scatter_start(s, tower):
        def hop(j, k, wide, way):
            return send(
                s.other.at[tower, wide * 4 + (y + k) % 4],
                s.round_in.at[tower, j],
                s.sem.at[0, tower, j],
                s.sem.at[1, tower, j],
                to_y(way),
            )

        s.relay[tower] = [hop(0, 2, 0, 1), hop(1, 2, 1, -1)]
        s.cross[tower] = send(
            s.one.at[tower, pl.ds((1 - low) * 4, 4)],
            s.cross_in.at[tower],
            s.sem.at[0, tower, 6],
            s.sem.at[1, tower, 6],
            partner,
        )
        s.near[tower] = [hop(2, 1, 1, 1), hop(3, 3, 0, -1)]

    def half_sum(s, tower, k):
        place = (y + k) % 4
        return s.one[tower, low * 4 + place].astype(F32) + s.cross_in[tower, place].astype(F32)

    def scatter_relay(s, tower):
        s.last[tower] = []
        for j, way in ((0, 1), (1, -1)):
            s.relay[tower][j].wait_recv()
            total = s.other[tower, j * 4 + (y + way) % 4].astype(F32)
            total += s.round_in[tower, j].astype(F32)
            s.round_out[tower, j] = total.astype(BF16)
            s.last[tower].append(
                send(
                    s.round_out.at[tower, j],
                    s.round_in.at[tower, 4 + j],
                    s.sem.at[0, tower, 4 + j],
                    s.sem.at[1, tower, 4 + j],
                    to_y(way),
                )
            )

    def scatter_along(s, tower):
        s.cross[tower].wait_recv()
        s.along[tower] = []
        for k in (2, 1, 3):
            s.half_out[tower, k] = half_sum(s, tower, k).astype(BF16)
            s.along[tower].append(
                send(
                    s.half_out.at[tower, k],
                    s.half_in.at[tower, k],
                    s.sem.at[0, tower, 7 + k],
                    s.sem.at[1, tower, 7 + k],
                    to_y(k),
                )
            )

    def scatter_wide(s, tower):
        for j in range(2):
            s.near[tower][1 - j].wait_recv()
            s.last[tower][j].wait_recv()
            total = s.other[tower, j * 4 + y].astype(F32)
            total += s.round_in[tower, 3 - j].astype(F32)
            total += s.round_in[tower, 4 + j].astype(F32)
            s.wide_out[tower, j] = total.astype(BF16)
        s.wide[tower] = send(
            s.wide_out.at[tower, 1 - low],
            s.wide_in.at[tower],
            s.sem.at[0, tower, 11],
            s.sem.at[1, tower, 11],
            partner,
        )

    def scatter_end(s, tower, axis):
        first = half_sum(s, tower, 0)
        for k in (1, 3, 2):
            s.along[tower][(2, 1, 3).index(k)].wait_recv()
            first += s.half_in[tower, k].astype(F32)
        s.wide[tower].wait_recv()
        second = s.wide_out[tower, low].astype(F32) + s.wide_in[tower].astype(F32)
        return jnp.concatenate([first, second], axis=axis)

    def down_projection(tower):
        loads[tower][0].wait()
        for f in range(4):
            loads[tower][1 + f].wait()
            product = jnp.dot(
                v.act[tower], v.w[tower, :, f * 384 : f * 384 + 384], preferred_element_type=F32
            )
            product = product.T.reshape(2, 192, 256).astype(BF16)
            v.down.one[tower, 2 * f : 2 * f + 2] = product[:, :80]
            v.down.other[tower, 2 * f : 2 * f + 2] = product[:, 80:]

        if tower == 1:
            pl.semaphore_wait(barrier, len(peers))
        scatter_start(v.down, tower)

    source = lax.broadcasted_iota(jnp.int32, (256, 256), 0)
    target = lax.broadcasted_iota(jnp.int32, (256, 256), 1)
    wanted = (target & 112) * 2 + (target & 15) + lax.shift_right_logical(target & 128, 3)
    reorder = (source == wanted).astype(F32).astype(BF16)

    def embedding_projection(tower):
        loads[tower][5].wait()
        loads[tower][6].wait()
        total = v.skip[tower].astype(F32) + scatter_end(v.down, tower, 0)
        columns = total.astype(BF16)
        rows = columns.T

        for f in range(6):
            product = jnp.dot(
                rows, v.m[tower, :, f * 256 : f * 256 + 256], preferred_element_type=F32
            )
            product = product.reshape(8, 32, 256).astype(BF16)
            cut = min(max(640 - f * 256, 0), 256)
            if cut > 0:
                v.emb.one[tower, :, :, f * 256 : f * 256 + cut] = product[:, :, :cut]
            if cut < 256:
                start = f * 256 + cut - 640
                v.emb.other[tower, :, :, start : start + 256 - cut] = product[:, :, cut:]

        scatter_start(v.emb, tower)
        v.stream[0, tower] = jnp.dot(columns, reorder, preferred_element_type=F32).astype(BF16)

    def await_all(copies):
        for copy in copies:
            copy.wait_recv()

    def stream_push(at, to, tower, way):
        sem = v.stream_sem
        return send(
            v.stream.at[at, tower],
            v.stream.at[to, tower],
            sem.at[0, to, tower],
            sem.at[1, to, tower],
            to_z(way),
        )

    def stream_step(step, tower):
        if step < 4:
            up = stream_push(step - 1, step, tower, 1)
            return [up, stream_push((9 - step) % 8, 8 - step, tower, -1)]
        return [stream_push(3, 4, 0, 1) if tower == 0 else stream_push(5, 4, 1, -1)]

    first, second = 1, 0
    down_projection(first)
    down_projection(second)
    scatter_relay(v.down, first)
    scatter_along(v.down, first)
    scatter_relay(v.down, second)
    scatter_wide(v.down, first)
    scatter_along(v.down, second)
    scatter_wide(v.down, second)
    stream_ring = {}
    embedding_projection(first)
    stream_ring[first] = stream_step(1, first)
    embedding_projection(second)
    stream_ring[second] = stream_step(1, second)

    def stream_next(step, tower):
        await_all(stream_ring[tower])
        stream_ring[tower] = stream_step(step, tower)

    scatter_relay(v.emb, first)
    scatter_along(v.emb, first)
    scatter_relay(v.emb, second)
    stream_next(2, first)
    scatter_wide(v.emb, first)
    stream_next(2, second)
    scatter_along(v.emb, second)
    scatter_wide(v.emb, second)

    def embed(tower):
        raw = scatter_end(v.emb, tower, 1)
        norm = jnp.sqrt(jnp.sum(raw * raw, axis=1, keepdims=True) + 1e-06)
        unit = raw / norm
        v.unit[tower] = unit
        v.norm[tower] = jnp.broadcast_to(norm, (32, 128))
        return unit.astype(BF16)

    mark = len(sends)
    v.txt[0, 0] = embed(1)
    pair_copies = []
    txt_copies = {}

    def share(slot):
        pair_copies.append(
            send(v.txt.at[0, slot], v.txt.at[1, slot], v.pair_sem.at[0, slot], v.pair_sem.at[1, slot], sibling)
        )

    def txt_step(step):
        up, down = (step - 1, step, 1), ((9 - step) % 8, 8 - step, -1)
        for (at, to, way), half in ((up, 0), (down, 1), (up, 1), (down, 0)):
            if at != 0:
                txt_copies[at, half].wait_recv()
            if to != 4 or half == (way < 0):
                rows = pl.ds(half * 16, 16)
                txt_copies[to, half] = send(
                    v.txt.at[0, at, rows],
                    v.txt.at[0, to, rows],
                    v.txt_sem.at[0, to, half],
                    v.txt_sem.at[1, to, half],
                    to_z(way),
                )
        for at in {up[0], down[0]}:
            share(at)

    txt_step(1)

    unit = embed(0)
    v.img[0, 0, 0] = unit[:16]
    v.img[1, 0, 0] = unit[16:]
    ways = (to_x, to_y)

    def image_push(at, to, phase, half, k, way):
        sem = v.img_sem
        return send(
            v.img.at[at], v.img.at[to], sem.at[0, phase, half, k], sem.at[1, phase, half, k], way(k)
        )

    img_first, img_copies = ([], []), {1: [], 2: [], 3: []}
    for k in (2, 1, 3):
        for half in range(2):
            img_first[half].append(image_push((half, 0, 0), (half, 0, k), 0, half, k, ways[half]))
    for k in (2, 1, 3):
        for half in range(2):
            img_copies[k].append(image_push((half, 0, 0), (half, k, 0), 1, half, k, ways[1 - half]))

    txt_step(2)
    txt_step(3)
    turned = pl.ds(1, 3)
    for half in range(2):
        await_all(img_first[half])
        for k in (2, 1, 3):
            img_copies[k].append(
                image_push((half, 0, turned), (half, k, turned), 2, half, k, ways[1 - half])
            )
    txt_step(4)
    settle(mark)
    await_all(txt_copies[4, half] for half in range(2))
    share(4)
    stream_next(3, first)
    stream_next(3, second)
    mark = len(sends)

    scale, shift = scale_ref[0], shift_ref[0]
    row_id = lax.broadcasted_iota(jnp.int32, (256, 256), 0)
    col_id = lax.broadcasted_iota(jnp.int32, (256, 256), 1)

    own_pair = ((row_id < 16) & (col_id == row_id)) | (
        (row_id >= 128) & (row_id < 144) & (col_id == row_id - 112)
    )

    def pair_coefficients(core, group):
        inner = lax.dot_general(
            v.img[:, 2 * group : 2 * group + 2].reshape(256, 1536),
            v.txt[core].reshape(256, 1536),
            (((1,), (1,)), ((), ())),
            preferred_element_type=F32,
        )
        value = jax.nn.sigmoid(scale * inner + shift)
        if core == 0 and group == 0:
            value = value - own_pair.astype(F32)
        value = scale * value
        turned_value = value.T.astype(BF16)
        value = value.astype(BF16)
        for half in range(2):
            part = slice(half * 128, half * 128 + 128)
            start = group * 128
            v.coef[half, start : start + 128, core * 256 : core * 256 + 256] = value[part]
            v.coef_t[core, :, half * 256 + start : half * 256 + start + 128] = turned_value[:, part]

    await_all(img_copies[1] + img_copies[2] + img_copies[3])
    pair_coefficients(0, 0)
    pair_coefficients(0, 1)
    await_all(pair_copies)
    pair_coefficients(1, 0)
    pair_coefficients(1, 1)

    def text_partials(core):
        @pl.loop(0, 6, unroll=True)
        def _(f):
            cols = pl.ds(pl.multiple_of(f * 256, 256), 256)
            product = jnp.dot(
                v.coef_t[core], v.img[:, :, :, :, cols].reshape(512, 256), preferred_element_type=F32
            ).reshape(8, 32, 256)
            if core == 0:
                v.gt_own[:, :, cols] = product
            else:
                v.gt_out[:, :, cols] = product.astype(BF16)

    def image_partials(half):
        @pl.loop(0, 6, unroll=True)
        def _(f):
            cols = pl.ds(pl.multiple_of(f * 256, 256), 256)
            product = jnp.dot(
                v.coef[half], v.txt[:, :, :, cols].reshape(512, 256), preferred_element_type=F32
            )
            v.gi_out[half, :, :, :, cols] = product.reshape(4, 4, 16, 256).astype(BF16)

    gi_first, gi_copies = ([], []), ([], [])

    def image_start(half):
        image_partials(half)
        for phase, blocks, copies in ((0, turned, gi_first), (2, pl.ds(0, 1), gi_copies)):
            for k in (2, 1, 3):
                copies[half].append(
                    send(
                        v.gi_out.at[half, k, blocks],
                        v.gi_in.at[half, k, blocks],
                        v.gi_sem.at[0, phase, half, k],
                        v.gi_sem.at[1, phase, half, k],
                        ways[1 - half](-k),
                    )
                )

    gh_copies = ([], [])

    def image_own(half, k):
        total = v.gi_out[half, 0, k].astype(F32)
        for j in range(1, 4):
            total += v.gi_in[half, j, k].astype(F32)
        return total

    def image_middle(half):
        await_all(gi_first[half])
        for k in (2, 1, 3):
            v.gh_out[half, k] = image_own(half, k).astype(BF16)
            gh_copies[half].append(
                send(
                    v.gh_out.at[half, k],
                    v.gh_in.at[half, k],
                    v.gi_sem.at[0, 1, half, k],
                    v.gi_sem.at[1, 1, half, k],
                    ways[half](-k),
                )
            )

    def image_end(half):
        await_all(gi_copies[half])
        total = image_own(half, 0)
        await_all(gh_copies[half])
        for k in range(1, 4):
            total += v.gh_in[half, k].astype(F32)
        return total

    gz_copies = {}

    def text_own(r, half):
        rows = slice(half * 16, half * 16 + 16)
        return v.gt_own[r, rows] + v.gt_in[r, rows].astype(F32)

    def text_step(step):
        moves = [(5 - step, 0, -1), (3 + step, 1, 1)]
        if step < 4:
            moves += [(4 - step, 1, -1), (4 + step, 0, 1)]
        for r, half, way in moves:
            rows = slice(half * 16, half * 16 + 16)
            total = text_own(r, half)
            before = r - way
            if (before, half) in gz_copies and (before != 4 or half == (way > 0)):
                gz_copies[before, half].wait_recv()
                total += v.gz_in[before, rows].astype(F32)
            v.gz_out[r, rows] = total.astype(BF16)
            gz_copies[r, half] = send(
                v.gz_out.at[r, pl.ds(half * 16, 16)],
                v.gz_in.at[r, pl.ds(half * 16, 16)],
                v.gz_sem.at[0, r, half],
                v.gz_sem.at[1, r, half],
                to_z(way),
            )

    def text_end(half):
        rows = slice(half * 16, half * 16 + 16)
        total = text_own(0, half)
        for r in (1, 7):
            gz_copies[r, half].wait_recv()
            total += v.gz_in[r, rows].astype(F32)
        return total

    text_partials(1)
    gt_copies = []
    for j, (start, count) in enumerate(((3, 3), (0, 3), (6, 2))):
        part = pl.ds(start, count)
        gt_copies.append(
            send(v.gt_out.at[part], v.gt_in.at[part], v.gt_sem.at[0, j], v.gt_sem.at[1, j], sibling)
        )
    text_partials(0)
    image_start(0)
    gt_copies[0].wait_recv()
    text_step(1)
    image_start(1)
    await_all(gt_copies[1:])
    settle(mark)
    text_step(2)
    text_step(3)
    image_middle(0)
    image_middle(1)
    text_step(4)
    mark = len(sends)

    turn_copies = ({}, {})

    def turn(tower, grad):
        raw = raw_gradient(grad, v.unit[tower], v.norm[tower][:, :1])
        for k in range(8):
            cols = slice(k * 192, k * 192 + 192)
            v.pack[tower, k] = jnp.concatenate([raw[:16, cols], raw[16:, cols]], axis=1)
        v.graw[tower, t, 0] = v.pack[tower, z]
        for k in (4, 3, 5, 2, 6, 1, 7):
            turn_copies[tower][k] = send(
                v.pack.at[tower, (z + k) % 8],
                v.graw.at[tower, t, k],
                v.turn_sem.at[0, tower, k],
                v.turn_sem.at[1, tower, k],
                to_z(k),
            )

    turn(1, jnp.concatenate([text_end(half) for half in range(2)], axis=0))
    turn(0, jnp.concatenate([image_end(half) for half in range(2)], axis=0))

    spread_copies, low_copies, high_copies = ([], []), {}, {}

    low_slots, high_slots = pl.ds(0, 3), pl.ds(3, 5)

    def spread(tower, owner, slots, phase, j, peer):
        block = v.graw.at[tower, owner, slots]
        sem = v.spread_sem
        return send(block, block, sem.at[0, tower, phase, j], sem.at[1, tower, phase, j], peer)

    def spread_start(tower):
        await_all(turn_copies[tower][k] for k in (1, 2))
        low_copies[tower] = spread(tower, t, low_slots, 0, 0, partner)
        await_all(turn_copies[tower][k] for k in range(3, 8))
        high_copies[tower] = {
            k: spread(tower, t, high_slots, 0, k, to_y(k)) for k in (2, 1, 3)
        }
        spread_copies[tower].append(spread(tower, t, high_slots, 1, 0, partner))
        spread_copies[tower].extend(
            spread(tower, t, low_slots, 1, k, to_y(k)) for k in (2, 1, 3)
        )

    def spread_end(tower):
        low_copies[tower].wait_recv()
        for k in (2, 1, 3):
            spread_copies[tower].append(
                spread(tower, (t + 4) % 8, low_slots, 2, k, to_y(k))
            )
        for k in (1, 3, 2):
            high_copies[tower][k].wait_recv()
            owner = low * 4 + (y - k) % 4
            spread_copies[tower].append(spread(tower, owner, high_slots, 2, k + 4, partner))

    def contract(tower):
        await_all(spread_copies[tower])
        totals = [jnp.zeros((192, 256), F32)] * 2
        for r in range(0, 8, 2):
            rows = jnp.concatenate([v.graw[tower, :, r + i].reshape(128, 384) for i in range(2)], axis=0)
            for half in range(2):
                lanes = slice(half * 128, half * 128 + 128)
                columns = jnp.concatenate([v.stream[r + i, tower, :, lanes] for i in range(2)], axis=1)
                totals[half] += jnp.dot(
                    columns, rows[:, half * 128 : half * 128 + 256], preferred_element_type=F32
                )
        total = totals[0][:, :192] + totals[1][:, 64:]
        return jnp.concatenate([total, jnp.zeros((64, 192), F32)], axis=0).T

    stream_next(4, first)
    stream_next(4, second)
    spread_start(first)
    spread_start(second)
    settle(mark)
    spread_end(first)
    spread_end(second)
    mark = len(sends)
    await_all(stream_ring[first] + stream_ring[second])

    high = x // 2
    core_copies, last_copies, totals = {}, {}, {}
    for tower in (first, second):
        columns = contract(tower)
        for q in range(4):
            v.part[tower, q % 2, q // 2] = columns[q * 48 : q * 48 + 48]
        core_copies[tower] = send(
            v.part.at[tower, 1 - c],
            v.part_in.at[tower],
            v.part_sem.at[0, tower, 0],
            v.part_sem.at[1, tower, 0],
            sibling,
        )
    for tower in (first, second):
        core_copies[tower].wait_recv()
        v.last_out[tower] = v.part[tower, c, 1 - high] + v.part_in[tower, 1 - high]
        last_copies[tower] = send(
            v.last_out.at[tower],
            v.last_in.at[tower],
            v.part_sem.at[0, tower, 1],
            v.part_sem.at[1, tower, 1],
            device(z, (x + 2) % 4, y, c),
        )
    settle(mark)
    for tower in (first, second):
        total = v.part[tower, c, high] + v.part_in[tower, high]
        last_copies[tower].wait_recv()
        totals[tower] = (total + v.last_in[tower])[:, :192]
    output[...] = jnp.concatenate([totals[0], totals[1]], axis=1)
    settle(len(sends))


def on_device(
    picture_skip_entries,
    picture_activations,
    picture_contract_weights,
    picture_embedding_map,
    caption_skip_entries,
    caption_activations,
    caption_contract_weights,
    caption_embedding_map,
    sharpness_coefficient,
    pairwise_score_shift,
):
    both = pl.pallas_call(
        window_kernel,
        out_shape=jax.ShapeDtypeStruct((48, 384), F32),
        in_specs=[pl.BlockSpec(memory_space=pl.ANY)] * 8
        + [pl.BlockSpec(memory_space=pltpu.SMEM)] * 2,
        out_specs=pl.BlockSpec(memory_space=pltpu.VMEM),
        scratch_shapes=[*SCRATCH.values(), *DOWN.values(), *EMB.values()],
        compiler_params=pltpu.CompilerParams(
            collective_id=0, has_side_effects=True, vmem_limit_bytes=VMEM_LIMIT
        ),
    )(
        picture_activations,
        picture_contract_weights,
        picture_embedding_map,
        picture_skip_entries.T,
        caption_activations,
        caption_contract_weights,
        caption_embedding_map,
        caption_skip_entries.T,
        sharpness_coefficient,
        pairwise_score_shift,
    )
    return both[:, :192].T, both[:, 192:].T


def solution(mesh):
    placed = (
        P("dp", "tensor"),
        P("dp", "tensor"),
        P("tensor", None),
        P("tensor", None),
        P("dp", "tensor"),
        P("dp", "tensor"),
        P("tensor", None),
        P("tensor", None),
        P(),
        P(),
    )
    return jax.shard_map(
        on_device,
        mesh=mesh,
        in_specs=placed,
        out_specs=(P("tensor", "dp"), P("tensor", "dp")),
        check_vma=False,
    )
```
